32 devices in a mesh: loop: 8 (over z, y), rep: 4 (over x, core).
Axes of the slice: x: 2, y: 2, z: 4, core: 2. Of those that a mesh axis runs over, the one named last changes fastest.
Arguments:
- features: bfloat16 [8192, 128], P(('loop', 'rep')), may hold values from -6 to 6
- w_self: bfloat16 [128, 256], replicated, may hold values from -0.5 to 0.5
- w_neigh: bfloat16 [128, 256], replicated, may hold values from -0.5 to 0.5
- bias: float32 [256], replicated, may hold values from -3 to 3
- degree: int32 [8192], P(('loop', 'rep')), may hold values from 1 to 4
- tiles: bfloat16 [8, 4, 8, 16, 128, 128], P('loop', 'rep'), may hold values from -0.09375 to 0.09375
- dst_block: int32 [8, 4, 8, 16], P('loop', 'rep'), may hold values from 0 to 7, as said below
- src_block: int32 [8, 4, 8, 16], P('loop', 'rep'), may hold values from 0 to 1, as said below
- live_count: int32 [8, 4, 8], P('loop', 'rep'), may hold values from 1 to 16, as said below
- cotangent: bfloat16 [8192, 256], P(('loop', 'rep')), may hold values from -6 to 6
Outputs:
- output: bfloat16 [8192, 256], P(('loop', 'rep'))
- grad_input: bfloat16 [8192, 128], P(('loop', 'rep'))
- grad_self: float32 [128, 256], replicated
- grad_neigh: float32 [128, 256], replicated
- grad_bias: float32 [256], replicated
The draws below stay inside these ranges and needn't reach their ends.
Inputs may be any that keep to these rules, and one draw needn't show every extreme that they name: Within one (p, r, q) the 16 slots name distinct pairs (dst_block, src_block). Within one (p, r, q) the 16 slots name distinct pairs (dst_block, src_block). `live_count`: every device (p, r) has some q with all 16 slots live; slots at or past the count hold tiles that are not part of the graph.
All inputs are finite; a program needn't handle non-finite values.
Results may differ from the reference program's by a relative error of at most 0.0075.
Values may be sent and summed in bfloat16 or wider, within the bound.
No kernel may reach another device: no remote copies, remote signals or barrier semaphores. Data moves between devices by JAX's collectives and lax.ppermute only.
A program may use at most 128 MiB of HBM per device.

```python
import math
import jax
import jax.numpy as jnp
from jax import lax

F = 128
H = 256
BLK = 128
SLOTS = 16
SUB_BLK = 2
NODES = 8192
N_LOOP = 8
N_REP = 4


def tile_pairs(key):
    base = jax.random.fold_in(key, 7)
    keys = jax.random.split(base, N_LOOP * N_REP * N_LOOP)
    candidates = SUB_BLK * SUB_BLK * N_REP
    picks = jax.vmap(lambda one_key: jax.random.permutation(one_key, candidates)[:SLOTS])(keys)
    return picks.reshape(N_LOOP, N_REP, N_LOOP, SLOTS).astype(jnp.int32)


def draw_dst_block(key, part):
    return tile_pairs(key) // SUB_BLK


def draw_src_block(key, part):
    return tile_pairs(key) % SUB_BLK


def draw_live_count(key, part):
    base = jax.random.fold_in(key, 11)
    key_level, key_raw, key_full = jax.random.split(base, 3)
    level = jax.random.randint(key_level, (N_LOOP, N_REP, 1), 1, SLOTS + 1)
    raw_counts = jax.random.randint(key_raw, (N_LOOP, N_REP, N_LOOP), 0, SLOTS * 4)
    counts = 1 + raw_counts % level
    full_part = jax.random.randint(key_full, (N_LOOP, N_REP, 1), 0, N_LOOP)
    positions = jnp.arange(N_LOOP)[None, None, :]
    return jnp.where(positions == full_part, SLOTS, counts).astype(jnp.int32)


def plant(array, own_key, low, top_value):
    index_at = [jax.random.randint(jax.random.fold_in(own_key, axis), (), 0, length) for axis, length in enumerate(array.shape)]
    main_axis = array.shape.index(max(array.shape))
    neighbour = index_at[:main_axis] + [(index_at[main_axis] + 1) % array.shape[main_axis]] + index_at[main_axis + 1:]
    return array.at[tuple(index_at)].set(low).at[tuple(neighbour)].set(top_value)


def levels(stream_key, dims, shards, low, top_value):
    factor_of = 1.0
    for dim, blocks in shards:
        steps = jax.random.uniform(jax.random.fold_in(jax.random.fold_in(stream_key, 6), dim), (blocks,), jnp.float32, low / len(shards), top_value / len(shards))
        factor_of = factor_of * jnp.repeat(jnp.exp(steps), dims[dim] // blocks).reshape((-1,) + (1,) * (len(dims) - 1 - dim))
    return factor_of


def bell_draw(key, extent, scale, limit, pieces=(), kind=jnp.bfloat16):
    drawn = jax.random.normal(key, extent, jnp.float32) * scale
    if len(pieces) > 0:
        drawn = levels(key, extent, pieces, -0.22, 0.18) * drawn
    return jnp.clip(drawn, min=-limit, max=limit).astype(kind)


def setup_inputs(seed: int = 0) -> dict:
    splits = jax.random.split(jax.random.key(seed), 11)
    features = bell_draw(splits[0], (NODES, F), 1.0, 6.0, ((0, 32),))
    w_self = bell_draw(splits[1], (F, H), F ** -0.5, 0.5)
    w_neigh = bell_draw(splits[2], (F, H), F ** -0.5, 0.5)
    bias = bell_draw(splits[3], (H,), 0.5, 3.0, (), jnp.float32)
    degree = plant(jax.random.randint(splits[4], (NODES,), 1, 5), jax.random.fold_in(splits[4], 1), 1, 4).astype(jnp.int32)
    tiles = bell_draw(splits[5], (N_LOOP, N_REP, N_LOOP, SLOTS, BLK, BLK), (BLK * N_LOOP * SLOTS // 4) ** -0.5, 0.09375, ((0, 8), (1, 4)))
    dst_block = draw_dst_block(jax.random.fold_in(splits[10], 71), 0)
    src_block = draw_src_block(jax.random.fold_in(splits[10], 71), 0)
    live_count = draw_live_count(jax.random.fold_in(splits[10], 71), 0)
    cotangent = bell_draw(splits[9], (NODES, H), 1.0, 6.0, ((0, 32),))
    return dict(features=features, w_self=w_self, w_neigh=w_neigh, bias=bias, degree=degree, tiles=tiles, dst_block=dst_block, src_block=src_block, live_count=live_count, cotangent=cotangent)


def reference(features, w_self, w_neigh, bias, degree, tiles, dst_block, src_block, live_count, cotangent):
    row_blocks = SUB_BLK * N_REP
    part_rows = row_blocks * BLK
    blocks = features.reshape(N_LOOP, N_REP, SUB_BLK, BLK, F)
    part_index = jnp.arange(N_LOOP)[None, :, None]
    rep_index = jnp.arange(N_REP)[:, None, None]
    slot_index = jnp.arange(SLOTS)[None, None, :]

    def forward_part(owner):
        tile_owner = tiles[owner].astype(jnp.float32)
        dst_owner = dst_block[owner]
        src_owner = src_block[owner]
        live_mask = (slot_index < live_count[owner][:, :, None]).astype(jnp.float32)
        chosen = blocks[part_index, rep_index, src_owner].astype(jnp.float32)
        product = jnp.einsum('rqtij,rqtjf->rqtif', tile_owner, chosen) * live_mask[..., None, None]
        summed = jax.ops.segment_sum(product.reshape(-1, BLK, F), dst_owner.reshape(-1), num_segments=row_blocks)
        return summed.reshape(part_rows, F)
    agg_sum = lax.map(forward_part, jnp.arange(N_LOOP)).reshape(NODES, F)
    degree_f = degree.astype(jnp.float32)[:, None]
    aggregate = (agg_sum / degree_f).astype(jnp.bfloat16)
    preact = jnp.dot(features, w_self, preferred_element_type=jnp.float32) + jnp.dot(aggregate, w_neigh, preferred_element_type=jnp.float32) + bias
    sigmoid_val = jax.nn.sigmoid(preact)
    output = (preact * sigmoid_val).astype(jnp.bfloat16)
    grad_pre = (cotangent.astype(jnp.float32) * sigmoid_val * (1.0 + preact * (1.0 - sigmoid_val))).astype(jnp.bfloat16)
    grad_scale = 1.0 / math.sqrt(NODES)
    grad_self = jnp.dot(features.T, grad_pre, preferred_element_type=jnp.float32) * grad_scale
    grad_neigh = jnp.dot(aggregate.T, grad_pre, preferred_element_type=jnp.float32) * grad_scale
    grad_bias = lax.optimization_barrier(jnp.sum(grad_pre.astype(jnp.float32), axis=0)) * grad_scale
    grad_agg = (jnp.dot(grad_pre, w_neigh.T, preferred_element_type=jnp.float32) / degree_f).astype(jnp.bfloat16)
    grad_blocks = grad_agg.reshape(N_LOOP, row_blocks, BLK, F)

    def backward_part(running, owner):
        tile_owner = tiles[owner].astype(jnp.float32)
        dst_owner = dst_block[owner]
        src_owner = src_block[owner]
        live_mask = (slot_index < live_count[owner][:, :, None]).astype(jnp.float32)
        chosen = grad_blocks[owner][dst_owner].astype(jnp.float32)
        product = jnp.einsum('rqtij,rqtif->rqtjf', tile_owner, chosen) * live_mask[..., None, None]
        running = running.at[part_index, rep_index, src_owner].add(product)
        return (running, None)
    start = jnp.zeros((N_LOOP, N_REP, SUB_BLK, BLK, F), jnp.float32)
    neigh_grad, _ = lax.scan(backward_part, start, jnp.arange(N_LOOP))
    self_grad = jnp.dot(grad_pre, w_self.T, preferred_element_type=jnp.float32)
    grad_input = (self_grad + neigh_grad.reshape(NODES, F)).astype(jnp.bfloat16)
    return (output, grad_input, grad_self, grad_neigh, grad_bias)
```

```python
import functools
import math

import jax
import jax.numpy as jnp
from jax import lax
from jax.experimental import pallas as pl
from jax.experimental.pallas import tpu as pltpu
from jax.sharding import PartitionSpec as P

VMEM = pl.BlockSpec(memory_space=pltpu.VMEM)
SMEM = pl.BlockSpec(memory_space=pltpu.SMEM)


def swap(block, axis, mask):
    return lax.ppermute(block, axis, [(i, i ^ mask) for i in range(lax.axis_size(axis))])


def call(kernel, out_shape, in_specs, args, flops=0):
    moved = sum(a.size * a.dtype.itemsize for a in (*args, *out_shape))
    return pl.pallas_call(
        kernel,
        out_shape=list(out_shape),
        in_specs=in_specs,
        out_specs=[VMEM] * len(out_shape),
        compiler_params=pltpu.CompilerParams(vmem_limit_bytes=moved + (12 << 20)),
        cost_estimate=pl.CostEstimate(flops=flops, bytes_accessed=moved, transcendentals=0),
    )(*args)


def f32(shape):
    return jax.ShapeDtypeStruct(shape, jnp.float32)


def bf16(shape):
    return jax.ShapeDtypeStruct(shape, jnp.bfloat16)


def place_kernel(order, rep_count, sub_blocks, here, dst, src, live, tiles, *mats):
    tile_size = tiles.shape[-1]
    loop_here, rep_here = here[0], here[1]
    for mat, mask in zip(mats, order):
        source = loop_here ^ mask
        mat[...] = jnp.zeros_like(mat)

        def put(slot, carry):
            block, column = dst[source, slot], src[source, slot]
            away = lax.div(block, sub_blocks) ^ rep_here
            panel = (away & 1) * (rep_count // 2) + lax.shift_right_logical(away, 1)
            row = panel * sub_blocks + lax.rem(block, sub_blocks)
            rows = pl.ds(pl.multiple_of(row * tile_size, tile_size), tile_size)
            columns = pl.ds(pl.multiple_of(column * tile_size, tile_size), tile_size)
            mat[rows, columns] = tiles[source, slot]
            return carry

        lax.fori_loop(0, live[source], put, 0)


def gather_kernel(count, first, last, *refs):
    mats, panels, rest = refs[:count], refs[count : 2 * count], refs[2 * count :]
    total_rows = mats[0].shape[0]
    half = total_rows // 2
    chunk = min(256, half)
    for at in range(0, total_rows, chunk):
        rows = slice(at, at + chunk)
        total = None if first else rest[0][rows, :]
        for mat, panel in zip(mats, panels):
            term = jnp.dot(mat[rows, :], panel[...], preferred_element_type=jnp.float32)
            total = term if total is None else total + term
        if not last:
            rest[-1][rows, :] = total
        elif at < half:
            rest[-2][rows, :] = total
        else:
            rest[-1][at - half : at - half + chunk, :] = total.astype(jnp.bfloat16)


def self_kernel(features, w_self, bias, out):
    out[...] = (
        jnp.dot(features[...], w_self[...], preferred_element_type=jnp.float32) + bias[...]
    )


def middle_kernel(
    row_count, total, term, degree, own_part, cotangent, w_neigh, output, grad_pre, aggregate, grad_agg
):
    rows_all = total.shape[0]
    for at in range(0, rows_all, row_count):
        rows = slice(at, at + row_count)
        degree_f = degree[rows, :].astype(jnp.float32)
        agg = (
            (total[rows, :].astype(jnp.float32) + term[rows, :].astype(jnp.float32)) / degree_f
        ).astype(jnp.bfloat16)
        aggregate[rows, :] = agg
        preact = own_part[rows, :] + jnp.dot(
            agg, w_neigh[...], preferred_element_type=jnp.float32
        )
        sigmoid_val = jax.nn.sigmoid(preact)
        if at == 0:
            output[...] = (preact * sigmoid_val).astype(jnp.bfloat16)
        grad = (
            cotangent[rows, :].astype(jnp.float32)
            * sigmoid_val
            * (1.0 + preact * (1.0 - sigmoid_val))
        ).astype(jnp.bfloat16)
        grad_pre[rows, :] = grad
        back = lax.dot_general(
            grad, w_neigh[...], (((1,), (1,)), ((), ())), preferred_element_type=jnp.float32
        )
        grad_agg[rows, :] = (back / degree_f).astype(jnp.bfloat16)


def weight_kernel(scale, row_count, here, features, aggregate, grad_pre, w_self, keep, send, self_grad):
    first_core = (here[1] & 1) == 0
    parts = []
    for at in range(0, features.shape[0], row_count):
        rows = slice(at, at + row_count)
        grad = grad_pre[rows, :]
        grads = [
            lax.dot_general(
                a[rows, :], grad, (((0,), (0,)), ((), ())), preferred_element_type=jnp.float32
            )
            for a in (features, aggregate)
        ]
        parts.append((*grads, jnp.sum(grad.astype(jnp.float32), axis=0, keepdims=True)))
    while len(parts) > 1:
        parts = [
            tuple(x + y for x, y in zip(a, b)) for a, b in zip(parts[::2], parts[1::2])
        ]
    by_self, by_neigh, by_bias = (p * scale for p in parts[0])
    width = features.shape[1]
    for out, mine in ((keep, first_core), (send, jnp.logical_not(first_core))):
        out[:width, :] = jnp.where(mine, by_self, by_neigh)
        out[width:, :] = jnp.broadcast_to(by_bias, (out.shape[0] - width, by_bias.shape[1]))
    self_grad[...] = lax.dot_general(
        grad_pre[:row_count, :],
        w_self[...],
        (((1,), (1,)), ((), ())),
        preferred_element_type=jnp.float32,
    )


def spread_kernel(count, *refs):
    mats, (near, far), outs = refs[:count], refs[count : count + 2], refs[count + 2 :]
    half = near.shape[0]
    near_t, far_t = near[...].T, far[...].T
    for mat, out in zip(mats, outs):
        total = jnp.dot(near_t, mat[:half, :], preferred_element_type=jnp.float32)
        total += jnp.dot(far_t, mat[half:, :], preferred_element_type=jnp.float32)
        out[...] = total.T.astype(jnp.bfloat16)


def per_device(
    features, w_self, w_neigh, bias, degree, tiles, dst_block, src_block, live_count, cotangent
):
    loop_count = lax.axis_size("loop")
    rep_count = lax.axis_size("rep")
    row_count, feat_width = features.shape
    hidden = w_self.shape[1]
    tile_size = tiles.shape[-1]
    sub_blocks = row_count // tile_size
    all_rows = row_count * rep_count
    half_rows = all_rows // 2
    here = jnp.stack([lax.axis_index("loop"), lax.axis_index("rep")]).astype(jnp.int32)

    far_first = list(range(loop_count - 2, 0, -2))
    panels = {0: features}
    for mask in far_first:
        panels[mask] = swap(features, "loop", mask)
    for mask in (0, *far_first):
        panels[mask ^ 1] = swap(panels[mask], "loop", 1)

    degree_col = jnp.broadcast_to(degree.astype(jnp.bfloat16)[:, None], (row_count, feat_width))
    bundle = jnp.concatenate([features, degree_col, cotangent], axis=1)
    bundles = jnp.concatenate(
        [bundle] + [swap(bundle, "rep", mask) for mask in range(2, rep_count, 2)], axis=0
    )
    half_features = bundles[:, :feat_width]
    half_degree = bundles[:, feat_width : 2 * feat_width]
    half_cotangent = bundles[:, 2 * feat_width :]

    order = [m ^ low for m in (0, *far_first) for low in (0, 1)]
    placed = call(
        functools.partial(place_kernel, order, rep_count, sub_blocks),
        [bf16((all_rows, row_count))] * loop_count,
        [SMEM, SMEM, SMEM, SMEM, VMEM],
        (here, dst_block[0, 0], src_block[0, 0], live_count[0, 0], tiles[0, 0]),
    )
    mats = dict(zip(order, placed))
    (own_part,) = call(
        self_kernel,
        [f32((half_rows, hidden))],
        [VMEM] * 3,
        (half_features, w_self, bias[None, :]),
    )

    late = [m ^ 1 for m in far_first]
    early = [m for m in order if m not in late]

    def gather(masks, extra, out_shape, first, last):
        args = [mats[m] for m in masks] + [panels[m] for m in masks] + extra
        return call(
            functools.partial(gather_kernel, len(masks), first, last),
            out_shape,
            [VMEM] * len(args),
            args,
            flops=2 * len(masks) * all_rows * row_count * feat_width,
        )

    (running,) = gather(early, [], [f32((all_rows, feat_width))], True, False)
    keep, send = gather(
        late,
        [running],
        [f32((half_rows, feat_width)), bf16((half_rows, feat_width))],
        False,
        True,
    )
    total = (keep + swap(send, "rep", 1).astype(jnp.float32)).astype(jnp.bfloat16)
    mask = 2
    while True:
        blocks = total.reshape(-1, 2, mask // 2 * row_count, feat_width)
        term = swap(blocks[:, ::-1].reshape(half_rows, feat_width), "rep", mask)
        mask *= 2
        if mask >= rep_count:
            break
        total = (total.astype(jnp.float32) + term.astype(jnp.float32)).astype(jnp.bfloat16)

    output, grad_pre, aggregate, grad_agg = call(
        functools.partial(middle_kernel, row_count),
        [
            bf16((row_count, hidden)),
            bf16((half_rows, hidden)),
            bf16((half_rows, feat_width)),
            bf16((half_rows, feat_width)),
        ],
        [VMEM] * 6,
        (total, term, half_degree, own_part, half_cotangent, w_neigh),
        flops=4 * half_rows * feat_width * hidden,
    )
    grad_far = swap(grad_agg, "rep", 1)

    scale = 1.0 / math.sqrt(row_count * loop_count * rep_count)
    pad = 16
    keep_w, send_w, self_grad = call(
        functools.partial(weight_kernel, scale, row_count),
        [f32((feat_width + pad, hidden))] * 2 + [f32((row_count, feat_width))],
        [SMEM] + [VMEM] * 4,
        (here, half_features, aggregate, grad_pre, w_self),
        flops=4 * half_rows * feat_width * hidden,
    )
    weights = keep_w + swap(send_w, "rep", 1)

    spread = call(
        functools.partial(spread_kernel, loop_count),
        [bf16((row_count, feat_width))] * loop_count,
        [VMEM] * (loop_count + 2),
        (*[mats[m] for m in order], grad_agg, grad_far),
        flops=2 * loop_count * all_rows * row_count * feat_width,
    )
    terms = dict(zip(order, spread))

    back = self_grad
    for mask in (*far_first, 0):
        pair = terms[mask].astype(jnp.float32) + swap(terms[mask ^ 1], "loop", 1).astype(
            jnp.float32
        )
        if mask:
            pair = swap(pair.astype(jnp.bfloat16), "loop", mask).astype(jnp.float32)
        back = back + pair
    grad_input = back.astype(jnp.bfloat16)

    mask = loop_count // 2
    while mask:
        sent = weights.astype(jnp.bfloat16)
        weights = sent.astype(jnp.float32) + swap(sent, "loop", mask).astype(jnp.float32)
        mask //= 2
    other = swap(weights[:feat_width], "rep", 1)
    mine = weights[:feat_width]
    first_core = (lax.axis_index("rep") & 1) == 0
    grad_self = jnp.where(first_core, mine, other)
    grad_neigh = jnp.where(first_core, other, mine)
    grad_bias = weights[feat_width]
    return (output, grad_input, grad_self, grad_neigh, grad_bias)


def solution(mesh):
    in_specs = (
        P(("loop", "rep"), None),
        P(),
        P(),
        P(),
        P(("loop", "rep")),
        P("loop", "rep", None, None, None, None),
        P("loop", "rep", None, None),
        P("loop", "rep", None, None),
        P("loop", "rep", None),
        P(("loop", "rep"), None),
    )
    out_specs = (P(("loop", "rep"), None), P(("loop", "rep"), None), P(), P(), P())
    return jax.shard_map(
        per_device, mesh=mesh, in_specs=in_specs, out_specs=out_specs, check_vma=False
    )
```

```python
import functools
import math

import jax
import jax.numpy as jnp
from jax import lax
from jax.experimental import pallas as pl
from jax.experimental.pallas import tpu as pltpu
from jax.sharding import PartitionSpec as P

VMEM = pl.BlockSpec(memory_space=pltpu.VMEM)
HBM = pl.BlockSpec(memory_space=pltpu.HBM)


def swap(block, axis, mask):
    return lax.ppermute(block, axis, [(i, i ^ mask) for i in range(lax.axis_size(axis))])


def grant(held):
    return min(held + (4 << 20), 56 << 20)


def call(kernel, out_shape, in_specs, args, flops=0):
    moved = sum(math.prod(a.shape) * a.dtype.itemsize for a in (*args, *out_shape))
    return pl.pallas_call(
        kernel,
        out_shape=list(out_shape),
        in_specs=in_specs,
        out_specs=[VMEM] * len(out_shape),
        compiler_params=pltpu.CompilerParams(vmem_limit_bytes=grant(moved)),
        cost_estimate=pl.CostEstimate(flops=flops, bytes_accessed=moved, transcendentals=0),
    )(*args)


def after(value, *earlier):
    return lax.optimization_barrier((value, *earlier))


def in_hbm(value):
    return pltpu.with_memory_space_constraint(value, pltpu.HBM)


def f32(shape):
    return jax.ShapeDtypeStruct(shape, jnp.float32)


def bf16(shape):
    return jax.ShapeDtypeStruct(shape, jnp.bfloat16)


def place_kernel(
    near_count, order, rep_count, sub_blocks, packs, dst_far, src_far, live_far, tiles, *refs
):
    count = len(order)
    sides, refs = (refs[:3], refs[3:]) if packs else ((), refs)
    mats, refs = refs[:count], refs[count:]
    if packs:
        bundle, refs = refs[0], refs[1:]
    dst, src, live, stage, degree, read, done, left = refs
    tile_size = tiles.shape[-1]
    loop_here, rep_here = lax.axis_index("loop"), lax.axis_index("rep")
    moves = [(dst_far, dst), (src_far, src), (live_far, live)]
    if packs:
        width = sides[0].shape[1]
        moves += [
            (sides[1], degree),
            (sides[0], bundle.at[:, pl.ds(0, width)]),
            (sides[2], bundle.at[:, pl.ds(2 * width, bundle.shape[1] - 2 * width)]),
        ]
    moves = [pltpu.make_async_copy(far, near, read.at[k]) for k, (far, near) in enumerate(moves)]
    for move in moves:
        move.start()
    built = [mats[k] if k < near_count else stage.at[k - near_count] for k in range(count)]

    def copy(k, source, slot, row, column):
        rows = pl.ds(pl.multiple_of(row * tile_size, tile_size), tile_size)
        columns = pl.ds(pl.multiple_of(column * tile_size, tile_size), tile_size)
        return pltpu.make_async_copy(
            tiles.at[source, slot], built[k].at[rows, columns], done.at[k]
        )

    backward = list(reversed(range(count)))
    for k in backward:
        built[k][...] = jnp.zeros(built[k].shape, jnp.bfloat16)
        if k == count - 1:
            for move in moves[:3]:
                move.wait()
        source = loop_here ^ order[k]

        def put(slot, carry):
            block, column = dst[source, slot], src[source, slot]
            away = lax.div(block, sub_blocks) ^ rep_here
            panel = (away & 1) * (rep_count // 2) + lax.shift_right_logical(away, 1)
            row = panel * sub_blocks + lax.rem(block, sub_blocks)
            copy(k, source, slot, row, column).start()
            return carry

        lax.fori_loop(0, live[0, source], put, 0)
    if packs:
        for move in moves[3:]:
            move.wait()
        degree_f = jnp.broadcast_to(degree[...].astype(jnp.float32), (width, bundle.shape[0]))
        bundle[:, width : 2 * width] = degree_f.T.astype(jnp.bfloat16)
    for k in backward:

        def finish(slot, carry):
            copy(k, 0, 0, 0, 0).wait()
            return carry

        lax.fori_loop(0, live[0, loop_here ^ order[k]], finish, 0)
        if k >= near_count:
            pltpu.make_async_copy(built[k], mats[k], left.at[k - near_count]).start()
    for k in range(near_count, count):
        pltpu.make_async_copy(built[k], mats[k], left.at[k - near_count]).wait()


def fetched(mats, near_count, stage, done):
    fetches = []
    for k, mat in enumerate(mats[near_count:]):
        half = mat.shape[0] // 2
        for part in range(2):
            rows = pl.ds(part * half, half)
            fetches.append(
                pltpu.make_async_copy(mat.at[rows], stage.at[k, rows], done.at[2 * k + part])
            )
    for fetch in fetches:
        fetch.start()

    def take(j):
        if j < near_count:
            return mats[j]
        for fetch in fetches[2 * (j - near_count) : 2 * (j - near_count) + 2]:
            fetch.wait()
        return stage.at[j - near_count]

    return take


def gather_first_kernel(near_count, count, *refs):
    mats, panels, (out, stage, done) = refs[:count], refs[count:-3], refs[-3:]
    take = fetched(mats, near_count, stage, done)
    total_rows = out.shape[0]
    chunk = min(256, total_rows)
    for j, panel in enumerate(panels):
        mat = take(j)
        for at in range(0, total_rows, chunk):
            rows = slice(at, at + chunk)
            term = jnp.dot(mat[rows, :], panel[...], preferred_element_type=jnp.float32)
            out[rows, :] = term if j == 0 else out[rows, :] + term


def gather_last_kernel(count, *refs):
    mats, panels, (so_far, keep, send) = refs[:count], refs[count : 2 * count], refs[2 * count :]
    half = keep.shape[0]
    chunk = min(256, half)
    for at in range(0, 2 * half, chunk):
        rows = slice(at, at + chunk)
        total = so_far[rows, :]
        for mat, panel in zip(mats, panels):
            total += jnp.dot(mat[rows, :], panel[...], preferred_element_type=jnp.float32)
        if at < half:
            keep[rows, :] = total
        else:
            send[at - half : at - half + chunk, :] = total.astype(jnp.bfloat16)


def add_kernel(kept, arrived, *refs):
    out = refs[-1]
    out[...] = (kept[...].astype(jnp.float32) + arrived[...].astype(jnp.float32)).astype(out.dtype)


def middle_kernel(
    flip, scale, total, term, w_self, w_neigh, bias, *refs
):
    bundles, (output, grad_own, grad_agg, keep, send) = refs[:-5], refs[-5:]
    row_count, width = bundles[0].shape[0], w_neigh.shape[0]
    parts = []
    for j, bundle in enumerate(bundles):
        rows = slice(j * row_count, (j + 1) * row_count)
        there = slice((j ^ flip) * row_count, ((j ^ flip) + 1) * row_count)
        degree_f = bundle[:, width : width + 1].astype(jnp.float32)
        agg = (
            (total[rows, :].astype(jnp.float32) + term[there, :].astype(jnp.float32)) / degree_f
        ).astype(jnp.bfloat16)
        features = bundle[:, :width]
        preact = (
            jnp.dot(
                jnp.concatenate([features, agg], axis=1),
                jnp.concatenate([w_self[...], w_neigh[...]], axis=0),
                preferred_element_type=jnp.float32,
            )
            + bias[...]
        )
        sigmoid_val = jax.nn.sigmoid(preact)
        grad = (
            bundle[:, 2 * width :].astype(jnp.float32)
            * sigmoid_val
            * (1.0 + preact * (1.0 - sigmoid_val))
        ).astype(jnp.bfloat16)
        if j == 0:
            output[...] = (preact * sigmoid_val).astype(jnp.bfloat16)
            grad_own[...] = grad
        back = lax.dot_general(
            grad, w_neigh[...], (((1,), (1,)), ((), ())), preferred_element_type=jnp.float32
        )
        grad_agg[rows, :] = (back / degree_f).astype(jnp.bfloat16)
        grads = [
            lax.dot_general(
                a, grad, (((0,), (0,)), ((), ())), preferred_element_type=jnp.float32
            )
            for a in (features, agg)
        ]
        parts.append((*grads, jnp.sum(grad.astype(jnp.float32), axis=0, keepdims=True)))
    while len(parts) > 1:
        parts = [
            tuple(x + y for x, y in zip(a, b)) for a, b in zip(parts[::2], parts[1::2])
        ]
    by_self, by_neigh, by_bias = (p * scale for p in parts[0])
    first = (lax.axis_index("rep") & 1) == 0
    for out, mine in ((keep, first), (send, jnp.logical_not(first))):
        out[:width, :] = jnp.where(mine, by_self, by_neigh)
        out[width:, :] = jnp.broadcast_to(by_bias, (out.shape[0] - width, by_bias.shape[1]))


def spread(mat, near_t, far_t):
    half = near_t.shape[1]
    total = jnp.dot(near_t, mat[:half, :], preferred_element_type=jnp.float32)
    total += jnp.dot(far_t, mat[half:, :], preferred_element_type=jnp.float32)
    return total.T


def spread_away_kernel(groups, *refs):
    count = sum(groups)
    mats, (near, far), outs = refs[:count], refs[count : count + 2], refs[count + 2 :]
    near_t, far_t = near[...].T, far[...].T
    j = 0
    for size, out in zip(groups, outs):
        rows = out.shape[0] // size
        for k in range(size):
            term = spread(mats[j], near_t, far_t)
            out[k * rows : (k + 1) * rows, :] = term.astype(jnp.bfloat16)
            j += 1


def spread_here_kernel(near_count, count, *refs):
    mats, (near, far, grad_own, w_self) = refs[:count], refs[count : count + 4]
    outs, (stage, done) = refs[count + 4 : -2], refs[-2:]
    take = fetched(mats, near_count, stage, done)
    near_t, far_t = near[...].T, far[...].T
    for j, out in enumerate(outs):
        term = spread(take(j), near_t, far_t)
        if j == count - 1:
            term += lax.dot_general(
                grad_own[...],
                w_self[...],
                (((1,), (1,)), ((), ())),
                preferred_element_type=jnp.float32,
            )
        out[...] = term.astype(out.dtype)


def pair_kernel(last_term, own_term, message, last, own):
    rows = last.shape[0]
    last[...] = (
        last_term[...].astype(jnp.float32) + message[:rows, :].astype(jnp.float32)
    ).astype(last.dtype)
    own[...] = own_term[...] + message[rows:, :].astype(jnp.float32)


def sum_kernel(own, *refs):
    arrived, out = refs[:-1], refs[-1]
    total = own[...]
    for term in arrived:
        total += term[...].astype(jnp.float32)
    out[...] = total.astype(out.dtype)


def finish_kernel(weights, other, grad_self, grad_neigh, grad_bias):
    width = grad_self.shape[0]
    first = (lax.axis_index("rep") & 1) == 0
    mine = weights[:width, :]
    grad_self[...] = jnp.where(first, mine, other[...])
    grad_neigh[...] = jnp.where(first, other[...], mine)
    grad_bias[...] = weights[width : width + 1, :]


def added(kept, arrived, *earlier, dtype=jnp.bfloat16):
    (total,) = call(
        add_kernel,
        [jax.ShapeDtypeStruct(kept.shape, dtype)],
        [VMEM] * 2 + [pl.BlockSpec(memory_space=pl.ANY)] * len(earlier),
        (kept, arrived, *earlier),
    )
    return total


def per_device(
    features, w_self, w_neigh, bias, degree, tiles, dst_block, src_block, live_count, cotangent
):
    loop_count = lax.axis_size("loop")
    rep_count = lax.axis_size("rep")
    row_count, feat_width = features.shape
    hidden = w_self.shape[1]
    tile_size = tiles.shape[-1]
    sub_blocks = row_count // tile_size
    all_rows = row_count * rep_count
    half_rows = all_rows // 2

    far_first = list(range(loop_count - 2, 0, -2))
    panels = {0: features}
    for mask in (*far_first, 1):
        panels[mask] = swap(features, "loop", mask)

    mat_shape = (all_rows, row_count)
    mat_bytes = 2 * all_rows * row_count
    small = loop_count * mat_bytes <= 8 << 20
    late = [m ^ 1 for m in far_first]
    stay = [*far_first, 0]
    far_count = 0 if small else len(stay)
    graph = (dst_block[0, 0], src_block[0, 0], live_count[0], tiles[0, 0])
    sides = (features, degree[None, :], cotangent)

    def place(masks, far, packs):
        near_count = 0 if far else len(masks)
        kind = pltpu.HBM if far else jax.ShapeDtypeStruct
        bundle = [bf16((row_count, 2 * feat_width + hidden))] if packs else []
        operands = graph + sides if packs else graph
        placed = pl.pallas_call(
            functools.partial(place_kernel, near_count, masks, rep_count, sub_blocks, packs),
            out_shape=[kind(mat_shape, jnp.bfloat16)] * len(masks) + bundle,
            in_specs=[HBM] * len(operands),
            out_specs=[HBM if far else VMEM] * len(masks) + [VMEM] * len(bundle),
            scratch_shapes=[pltpu.SMEM(g.shape, jnp.int32) for g in graph[:3]]
            + [
                pltpu.VMEM((len(masks), *mat_shape) if far else (1, 16, 128), jnp.bfloat16),
                pltpu.VMEM((1, row_count), jnp.int32),
                pltpu.SemaphoreType.DMA((6,)),
                pltpu.SemaphoreType.DMA((len(masks),)),
                pltpu.SemaphoreType.DMA((len(masks),)),
            ],
            compiler_params=pltpu.CompilerParams(vmem_limit_bytes=grant(len(masks) * mat_bytes)),
            cost_estimate=pl.CostEstimate(
                flops=0, bytes_accessed=2 * len(masks) * mat_bytes, transcendentals=0
            ),
        )(*map(in_hbm, operands))
        mats = [in_hbm(mat) if far else mat for mat in placed[: len(masks)]]
        return dict(zip(masks, mats)), placed[len(masks) :]

    away_masks = [*late, 1]
    mats, (bundle,) = place(away_masks + stay if small else away_masks, False, True)
    if not small:
        mats |= place(stay, True, False)[0]
    bundles = [bundle] + [swap(bundle, "rep", mask) for mask in range(2, rep_count, 2)]
    arrivals = [*far_first, 1]
    mats[late[0]], *got = after(mats[late[0]], *[panels[m] for m in arrivals])
    panels.update(zip(arrivals, got))
    for mask in far_first:
        panels[mask ^ 1] = swap(panels[mask], "loop", 1)

    early = [1, *stay]
    (running,) = pl.pallas_call(
        functools.partial(gather_first_kernel, len(early) - far_count, len(early)),
        out_shape=[f32((all_rows, feat_width))],
        in_specs=[VMEM] * (len(early) - far_count)
        + [HBM] * far_count
        + [VMEM] * len(early),
        out_specs=[VMEM],
        scratch_shapes=[
            pltpu.VMEM((far_count, *mat_shape) if far_count else (1, 16, 128), jnp.bfloat16),
            pltpu.SemaphoreType.DMA((2 * max(1, far_count),)),
        ],
        compiler_params=pltpu.CompilerParams(vmem_limit_bytes=grant(2 * loop_count * mat_bytes)),
        cost_estimate=pl.CostEstimate(
            flops=2 * len(early) * all_rows * row_count * feat_width,
            bytes_accessed=far_count * mat_bytes,
            transcendentals=0,
        ),
    )(*[mats[m] for m in early], *[panels[m] for m in early])
    keep, send = call(
        functools.partial(gather_last_kernel, len(late)),
        [f32((half_rows, feat_width)), bf16((half_rows, feat_width))],
        [VMEM] * (2 * len(late) + 1),
        [mats[m] for m in late] + [panels[m] for m in late] + [running],
        flops=2 * len(late) * all_rows * row_count * feat_width,
    )
    total = added(keep, swap(send, "rep", 1))
    total, *bundles = after(total, *bundles)
    mask = 2
    while True:
        term = swap(total, "rep", mask)
        if 2 * mask >= rep_count:
            break
        blocks = term.reshape(-1, 2, mask // 2 * row_count, feat_width)[:, ::-1]
        total = (
            total.astype(jnp.float32) + blocks.reshape(half_rows, feat_width).astype(jnp.float32)
        ).astype(jnp.bfloat16)
        mask *= 2

    scale = 1.0 / math.sqrt(row_count * loop_count * rep_count)
    weight_shape = (feat_width + 16, hidden)
    output_shape = (row_count, hidden)
    output, grad_own, grad_agg, keep_w, send_w = call(
        functools.partial(middle_kernel, mask // 2, scale),
        [
            pltpu.VMEM(output_shape, jnp.bfloat16) if small else bf16(output_shape),
            bf16(output_shape),
            bf16((half_rows, feat_width)),
            f32(weight_shape),
            f32(weight_shape),
        ],
        [VMEM] * (5 + len(bundles)),
        (total, term, w_self, w_neigh, bias[None, :], *bundles),
        flops=8 * half_rows * feat_width * hidden,
    )
    grad_far = swap(grad_agg, "rep", 1)
    arrived_w = swap(send_w, "rep", 1)

    away_groups = [1] * (len(far_first) - 1) + [2]
    away = call(
        functools.partial(spread_away_kernel, away_groups),
        [bf16((size * row_count, feat_width)) for size in away_groups],
        [VMEM] * (len(stay) + 2),
        (*[mats[m] for m in away_masks], grad_agg, grad_far),
        flops=2 * len(stay) * all_rows * row_count * feat_width,
    )
    arrived = [swap(message, "loop", 1) for message in away]
    grad_far, *away = after(grad_far, *away)
    kept = pl.pallas_call(
        functools.partial(spread_here_kernel, len(stay) - far_count, len(stay)),
        out_shape=[bf16((row_count, feat_width))] * len(far_first)
        + [f32((row_count, feat_width))],
        in_specs=[VMEM] * (len(stay) - far_count) + [HBM] * far_count + [VMEM] * 4,
        out_specs=[VMEM] * len(stay),
        scratch_shapes=[
            pltpu.VMEM((far_count, *mat_shape) if far_count else (1, 16, 128), jnp.bfloat16),
            pltpu.SemaphoreType.DMA((2 * max(1, far_count),)),
        ],
        compiler_params=pltpu.CompilerParams(vmem_limit_bytes=grant(2 * loop_count * mat_bytes)),
        cost_estimate=pl.CostEstimate(
            flops=2 * len(stay) * all_rows * row_count * feat_width,
            bytes_accessed=far_count * mat_bytes,
            transcendentals=0,
        ),
    )(*[mats[m] for m in stay], grad_agg, grad_far, grad_own, w_self)
    back = [
        swap(added(term, message), "loop", m)
        for m, term, message in zip(far_first[:-1], kept, arrived)
    ]
    last, own = call(
        pair_kernel,
        [bf16((row_count, feat_width)), f32((row_count, feat_width))],
        [VMEM] * 3,
        (*kept[-2:], arrived[-1]),
    )
    back.append(swap(last, "loop", far_first[-1]))
    (grad_input,) = call(
        sum_kernel,
        [bf16((row_count, feat_width))],
        [VMEM] * (1 + len(back)),
        (own, *back),
        flops=4_000_000_000,
    )
    sent_w = added(keep_w, arrived_w)
    mask = loop_count // 2
    while mask:
        arrived_w = swap(sent_w, "loop", mask)
        dtype = jnp.bfloat16 if mask > 1 else jnp.float32
        earlier = [own] if mask == loop_count // 4 else []
        sent_w = added(sent_w, arrived_w, *earlier, dtype=dtype)
        mask //= 2
    other = swap(sent_w[:feat_width], "rep", 1)
    grad_self, grad_neigh, grad_bias = call(
        finish_kernel,
        [f32((feat_width, hidden)), f32((feat_width, hidden)), f32((1, hidden))],
        [VMEM] * 2,
        (sent_w, other),
    )
    return (output, grad_input, grad_self, grad_neigh, grad_bias[0])


def solution(mesh):
    in_specs = (
        P(("loop", "rep"), None),
        P(),
        P(),
        P(),
        P(("loop", "rep")),
        P("loop", "rep", None, None, None, None),
        P("loop", "rep", None, None),
        P("loop", "rep", None, None),
        P("loop", "rep", None),
        P(("loop", "rep"), None),
    )
    out_specs = (P(("loop", "rep"), None), P(("loop", "rep"), None), P(), P(), P())
    return jax.shard_map(
        per_device, mesh=mesh, in_specs=in_specs, out_specs=out_specs, check_vma=False
    )
```

```python
import functools
import math

import jax
import jax.numpy as jnp
from jax import lax
from jax.experimental import pallas as pl
from jax.experimental.pallas import tpu as pltpu
from jax.sharding import PartitionSpec as P

VMEM = pl.BlockSpec(memory_space=pltpu.VMEM)
HBM = pl.BlockSpec(memory_space=pltpu.HBM)


def swap(block, axis, mask):
    return lax.ppermute(block, axis, [(i, i ^ mask) for i in range(lax.axis_size(axis))])


def grant(held):
    return min(held + (4 << 20), 56 << 20)


def call(kernel, out_shape, in_specs, args, flops=0):
    moved = sum(math.prod(a.shape) * a.dtype.itemsize for a in (*args, *out_shape))
    return pl.pallas_call(
        kernel,
        out_shape=list(out_shape),
        in_specs=in_specs,
        out_specs=[VMEM] * len(out_shape),
        compiler_params=pltpu.CompilerParams(vmem_limit_bytes=grant(moved)),
        cost_estimate=pl.CostEstimate(flops=flops, bytes_accessed=moved, transcendentals=0),
    )(*args)


def after(value, *earlier):
    return lax.optimization_barrier((value, *earlier))


def in_hbm(value):
    return pltpu.with_memory_space_constraint(value, pltpu.HBM)


def f32(shape):
    return jax.ShapeDtypeStruct(shape, jnp.float32)


def bf16(shape):
    return jax.ShapeDtypeStruct(shape, jnp.bfloat16)


def place_kernel(
    near_count, order, rep_count, sub_blocks, packs, dst_far, src_far, live_far, tiles, *refs
):
    count = len(order)
    sides, refs = (refs[:3], refs[3:]) if packs else ((), refs)
    mats, refs = refs[:count], refs[count:]
    if packs:
        bundle, refs = refs[0], refs[1:]
    dst, src, live, stage, degree, read, done, left = refs
    tile_size = tiles.shape[-1]
    loop_here, rep_here = lax.axis_index("loop"), lax.axis_index("rep")
    sub_bits = sub_blocks.bit_length() - 1
    moves = [(dst_far, dst), (src_far, src), (live_far, live)]
    if packs:
        width = sides[0].shape[1]
        moves += [
            (sides[1], degree),
            (sides[0], bundle.at[:, pl.ds(0, width)]),
            (sides[2], bundle.at[:, pl.ds(2 * width, bundle.shape[1] - 2 * width)]),
        ]
    moves = [pltpu.make_async_copy(far, near, read.at[k]) for k, (far, near) in enumerate(moves)]
    for move in moves:
        move.start()
    built = [mats[k] if k < near_count else stage.at[k - near_count] for k in range(count)]

    def copy(k, source, slot, row, column):
        rows = pl.ds(pl.multiple_of(row * tile_size, tile_size), tile_size)
        columns = pl.ds(pl.multiple_of(column * tile_size, tile_size), tile_size)
        return pltpu.make_async_copy(
            tiles.at[source, slot], built[k].at[rows, columns], done.at[k]
        )

    backward = list(reversed(range(count)))
    for k in backward:
        built[k][...] = jnp.zeros(built[k].shape, jnp.bfloat16)
        if k == count - 1:
            for move in moves[:3]:
                move.wait()
        source = loop_here ^ order[k]

        def put(slot, carry):
            block, column = dst[source, slot], src[source, slot]
            away = lax.shift_right_logical(block, sub_bits) ^ rep_here
            panel = (away & 1) * (rep_count // 2) + lax.shift_right_logical(away, 1)
            row = panel * sub_blocks + (block & (sub_blocks - 1))
            copy(k, source, slot, row, column).start()
            return carry

        lax.fori_loop(0, live[0, source], put, 0)
    if packs:
        for move in moves[3:]:
            move.wait()
        degree_f = jnp.broadcast_to(degree[...].astype(jnp.float32), (width, bundle.shape[0]))
        bundle[:, width : 2 * width] = degree_f.T.astype(jnp.bfloat16)
    for k in backward:

        def finish(slot, carry):
            copy(k, 0, 0, 0, 0).wait()
            return carry

        lax.fori_loop(0, live[0, loop_here ^ order[k]], finish, 0)
        if k >= near_count:
            pltpu.make_async_copy(built[k], mats[k], left.at[k - near_count]).start()
    for k in range(near_count, count):
        pltpu.make_async_copy(built[k], mats[k], left.at[k - near_count]).wait()


def fetched(mats, near_count, stage, done):
    fetches = []
    for k, mat in enumerate(mats[near_count:]):
        half = mat.shape[0] // 2
        for part in range(2):
            rows = pl.ds(part * half, half)
            fetches.append(
                pltpu.make_async_copy(mat.at[rows], stage.at[k, rows], done.at[2 * k + part])
            )
    for fetch in fetches:
        fetch.start()

    def take(j):
        if j < near_count:
            return mats[j]
        for fetch in fetches[2 * (j - near_count) : 2 * (j - near_count) + 2]:
            fetch.wait()
        return stage.at[j - near_count]

    return take


def gather_first_kernel(near_count, count, *refs):
    mats, panels, (out, stage, done) = refs[:count], refs[count:-3], refs[-3:]
    take = fetched(mats, near_count, stage, done)
    total_rows = out.shape[0]
    chunk = min(256, total_rows)
    for j, panel in enumerate(panels):
        mat = take(j)
        for at in range(0, total_rows, chunk):
            rows = slice(at, at + chunk)
            term = jnp.dot(mat[rows, :], panel[...], preferred_element_type=jnp.float32)
            out[rows, :] = term if j == 0 else out[rows, :] + term


def gather_last_kernel(count, *refs):
    mats, panels, (so_far, keep, send) = refs[:count], refs[count : 2 * count], refs[2 * count :]
    half = keep.shape[0]
    chunk = min(256, half)
    for at in range(0, 2 * half, chunk):
        rows = slice(at, at + chunk)
        total = so_far[rows, :]
        for mat, panel in zip(mats, panels):
            total += jnp.dot(mat[rows, :], panel[...], preferred_element_type=jnp.float32)
        if at < half:
            keep[rows, :] = total
        else:
            send[at - half : at - half + chunk, :] = total.astype(jnp.bfloat16)


def add_kernel(kept, arrived, *refs):
    out = refs[-1]
    out[...] = (kept[...].astype(jnp.float32) + arrived[...].astype(jnp.float32)).astype(out.dtype)


def middle_kernel(
    flip, scale, total, term, w_self, w_neigh, bias, *refs
):
    bundles, (output, grad_own, grad_agg, keep, send) = refs[:-5], refs[-5:]
    row_count, width = bundles[0].shape[0], w_neigh.shape[0]
    parts = []
    for j, bundle in enumerate(bundles):
        rows = slice(j * row_count, (j + 1) * row_count)
        there = slice((j ^ flip) * row_count, ((j ^ flip) + 1) * row_count)
        degree_f = bundle[:, width : width + 1].astype(jnp.float32)
        agg = (
            (total[rows, :].astype(jnp.float32) + term[there, :].astype(jnp.float32)) / degree_f
        ).astype(jnp.bfloat16)
        features = bundle[:, :width]
        preact = (
            jnp.dot(
                jnp.concatenate([features, agg], axis=1),
                jnp.concatenate([w_self[...], w_neigh[...]], axis=0),
                preferred_element_type=jnp.float32,
            )
            + bias[...]
        )
        sigmoid_val = jax.nn.sigmoid(preact)
        grad = (
            bundle[:, 2 * width :].astype(jnp.float32)
            * sigmoid_val
            * (1.0 + preact * (1.0 - sigmoid_val))
        ).astype(jnp.bfloat16)
        if j == 0:
            output[...] = (preact * sigmoid_val).astype(jnp.bfloat16)
            grad_own[...] = grad
        back = lax.dot_general(
            grad, w_neigh[...], (((1,), (1,)), ((), ())), preferred_element_type=jnp.float32
        )
        grad_agg[rows, :] = (back / degree_f).astype(jnp.bfloat16)
        grads = [
            lax.dot_general(
                a, grad, (((0,), (0,)), ((), ())), preferred_element_type=jnp.float32
            )
            for a in (features, agg)
        ]
        parts.append((*grads, jnp.sum(grad.astype(jnp.float32), axis=0, keepdims=True)))
    while len(parts) > 1:
        parts = [
            tuple(x + y for x, y in zip(a, b)) for a, b in zip(parts[::2], parts[1::2])
        ]
    by_self, by_neigh, by_bias = (p * scale for p in parts[0])
    first = (lax.axis_index("rep") & 1) == 0
    for out, mine in ((keep, first), (send, jnp.logical_not(first))):
        out[:width, :] = jnp.where(mine, by_self, by_neigh)
        out[width:, :] = jnp.broadcast_to(by_bias, (out.shape[0] - width, by_bias.shape[1]))


def spread(mat, near_t, far_t):
    half = near_t.shape[1]
    total = jnp.dot(near_t, mat[:half, :], preferred_element_type=jnp.float32)
    total += jnp.dot(far_t, mat[half:, :], preferred_element_type=jnp.float32)
    return total.T


def spread_away_kernel(groups, *refs):
    count = sum(groups)
    mats, (near, far), outs = refs[:count], refs[count : count + 2], refs[count + 2 :]
    near_t, far_t = near[...].T, far[...].T
    j = 0
    for size, out in zip(groups, outs):
        rows = out.shape[0] // size
        for k in range(size):
            term = spread(mats[j], near_t, far_t)
            out[k * rows : (k + 1) * rows, :] = term.astype(jnp.bfloat16)
            j += 1


def spread_here_kernel(near_count, count, *refs):
    mats, (near, far, grad_own, w_self) = refs[:count], refs[count : count + 4]
    outs, (stage, done) = refs[count + 4 : -2], refs[-2:]
    take = fetched(mats, near_count, stage, done)
    near_t, far_t = near[...].T, far[...].T
    for j, out in enumerate(outs):
        term = spread(take(j), near_t, far_t)
        if j == count - 1:
            term += lax.dot_general(
                grad_own[...],
                w_self[...],
                (((1,), (1,)), ((), ())),
                preferred_element_type=jnp.float32,
            )
        out[...] = term.astype(out.dtype)


def pair_kernel(part, term, message, *refs):
    out = refs[-1]
    rows = out.shape[0]
    piece = message[part * rows : (part + 1) * rows, :]
    out[...] = (term[...].astype(jnp.float32) + piece.astype(jnp.float32)).astype(out.dtype)


def sum_kernel(part, own, message, *refs):
    arrived, out = refs[:-1], refs[-1]
    rows = out.shape[0]
    total = own[...] + message[part * rows : (part + 1) * rows, :].astype(jnp.float32)
    for term in arrived:
        total += term[...].astype(jnp.float32)
    out[...] = total.astype(out.dtype)


def finish_kernel(weights, other, grad_self, grad_neigh, grad_bias):
    width = grad_self.shape[0]
    first = (lax.axis_index("rep") & 1) == 0
    mine = weights[:width, :]
    grad_self[...] = jnp.where(first, mine, other[...])
    grad_neigh[...] = jnp.where(first, other[...], mine)
    grad_bias[...] = weights[width : width + 1, :]


def token_kernel(*refs):
    refs[-1][...] = jnp.zeros(refs[-1].shape, jnp.float32)


def token(values, flops):
    (out,) = call(
        token_kernel,
        [f32((8, 128))],
        [pl.BlockSpec(memory_space=pl.ANY)] * len(values),
        values,
        flops=flops,
    )
    return out


def added(kept, arrived, *earlier, dtype=jnp.bfloat16):
    (total,) = call(
        add_kernel,
        [jax.ShapeDtypeStruct(kept.shape, dtype)],
        [VMEM] * 2 + [pl.BlockSpec(memory_space=pl.ANY)] * len(earlier),
        (kept, arrived, *earlier),
    )
    return total


def per_device(
    features, w_self, w_neigh, bias, degree, tiles, dst_block, src_block, live_count, cotangent
):
    loop_count = lax.axis_size("loop")
    rep_count = lax.axis_size("rep")
    row_count, feat_width = features.shape
    hidden = w_self.shape[1]
    tile_size = tiles.shape[-1]
    sub_blocks = row_count // tile_size
    all_rows = row_count * rep_count
    half_rows = all_rows // 2

    far_first = list(range(loop_count - 2, 0, -2))
    panels = {0: features}
    for mask in (*far_first, 1):
        panels[mask] = swap(features, "loop", mask)

    mat_shape = (all_rows, row_count)
    mat_bytes = 2 * all_rows * row_count
    small = loop_count * mat_bytes <= 8 << 20
    late = [m ^ 1 for m in far_first]
    stay = [*far_first, 0]
    far_count = 0 if small else len(stay)
    graph = (dst_block[0, 0], src_block[0, 0], live_count[0], tiles[0, 0])
    sides = (features, degree[None, :], cotangent)

    def place(masks, far, packs):
        near_count = 0 if far else len(masks)
        kind = pltpu.HBM if far else jax.ShapeDtypeStruct
        bundle = [bf16((row_count, 2 * feat_width + hidden))] if packs else []
        operands = graph + sides if packs else graph
        placed = pl.pallas_call(
            functools.partial(place_kernel, near_count, masks, rep_count, sub_blocks, packs),
            out_shape=[kind(mat_shape, jnp.bfloat16)] * len(masks) + bundle,
            in_specs=[HBM] * len(operands),
            out_specs=[HBM if far else VMEM] * len(masks) + [VMEM] * len(bundle),
            scratch_shapes=[pltpu.SMEM(g.shape, jnp.int32) for g in graph[:3]]
            + [
                pltpu.VMEM((len(masks), *mat_shape) if far else (1, 16, 128), jnp.bfloat16),
                pltpu.VMEM((1, row_count), jnp.int32),
                pltpu.SemaphoreType.DMA((6,)),
                pltpu.SemaphoreType.DMA((len(masks),)),
                pltpu.SemaphoreType.DMA((len(masks),)),
            ],
            compiler_params=pltpu.CompilerParams(vmem_limit_bytes=grant(len(masks) * mat_bytes)),
            cost_estimate=pl.CostEstimate(
                flops=0, bytes_accessed=2 * len(masks) * mat_bytes, transcendentals=0
            ),
        )(*map(in_hbm, operands))
        mats = [in_hbm(mat) if far else mat for mat in placed[: len(masks)]]
        return dict(zip(masks, mats)), placed[len(masks) :]

    away_masks = [*late, 1]
    mats, (bundle,) = place(away_masks + stay if small else away_masks, False, True)
    if not small:
        mats |= place(stay, True, False)[0]
    bundles = [bundle] + [swap(bundle, "rep", mask) for mask in range(2, rep_count, 2)]
    arrivals = [*far_first, 1]
    mats[late[0]], *got = after(mats[late[0]], *[panels[m] for m in arrivals])
    panels.update(zip(arrivals, got))
    for mask in far_first:
        panels[mask ^ 1] = swap(panels[mask], "loop", 1)

    early = [1, *stay]
    (running,) = pl.pallas_call(
        functools.partial(gather_first_kernel, len(early) - far_count, len(early)),
        out_shape=[f32((all_rows, feat_width))],
        in_specs=[VMEM] * (len(early) - far_count)
        + [HBM] * far_count
        + [VMEM] * len(early),
        out_specs=[VMEM],
        scratch_shapes=[
            pltpu.VMEM((far_count, *mat_shape) if far_count else (1, 16, 128), jnp.bfloat16),
            pltpu.SemaphoreType.DMA((2 * max(1, far_count),)),
        ],
        compiler_params=pltpu.CompilerParams(vmem_limit_bytes=grant(2 * loop_count * mat_bytes)),
        cost_estimate=pl.CostEstimate(
            flops=2 * len(early) * all_rows * row_count * feat_width,
            bytes_accessed=far_count * mat_bytes,
            transcendentals=0,
        ),
    )(*[mats[m] for m in early], *[panels[m] for m in early])
    keep, send = call(
        functools.partial(gather_last_kernel, len(late)),
        [f32((half_rows, feat_width)), bf16((half_rows, feat_width))],
        [VMEM] * (2 * len(late) + 1),
        [mats[m] for m in late] + [panels[m] for m in late] + [running],
        flops=2 * len(late) * all_rows * row_count * feat_width,
    )
    total = added(keep, swap(send, "rep", 1))
    total, *bundles = after(total, *bundles)
    mask = 2
    while True:
        term = swap(total, "rep", mask)
        if 2 * mask >= rep_count:
            break
        blocks = term.reshape(-1, 2, mask // 2 * row_count, feat_width)[:, ::-1]
        total = (
            total.astype(jnp.float32) + blocks.reshape(half_rows, feat_width).astype(jnp.float32)
        ).astype(jnp.bfloat16)
        mask *= 2

    scale = 1.0 / math.sqrt(row_count * loop_count * rep_count)
    weight_shape = (feat_width + 16, hidden)
    output_shape = (row_count, hidden)
    output, grad_own, grad_agg, keep_w, send_w = call(
        functools.partial(middle_kernel, mask // 2, scale),
        [
            pltpu.VMEM(output_shape, jnp.bfloat16) if small else bf16(output_shape),
            bf16(output_shape),
            bf16((half_rows, feat_width)),
            f32(weight_shape),
            f32(weight_shape),
        ],
        [VMEM] * (5 + len(bundles)),
        (total, term, w_self, w_neigh, bias[None, :], *bundles),
        flops=8 * half_rows * feat_width * hidden,
    )
    grad_far = swap(grad_agg, "rep", 1)
    sent_w = added(keep_w, swap(send_w, "rep", 1))

    away_groups = [1] * (len(far_first) - 1) + [2]
    away = call(
        functools.partial(spread_away_kernel, away_groups),
        [bf16((size * row_count, feat_width)) for size in away_groups],
        [VMEM] * (len(stay) + 2),
        (*[mats[m] for m in away_masks], grad_agg, grad_far),
        flops=2 * len(stay) * all_rows * row_count * feat_width,
    )
    arrived = [swap(message, "loop", 1) for message in away]
    grad_far, *away = after(grad_far, *away)
    kept = pl.pallas_call(
        functools.partial(spread_here_kernel, len(stay) - far_count, len(stay)),
        out_shape=[bf16((row_count, feat_width))] * len(far_first)
        + [f32((row_count, feat_width))],
        in_specs=[VMEM] * (len(stay) - far_count) + [HBM] * far_count + [VMEM] * 4,
        out_specs=[VMEM] * len(stay),
        scratch_shapes=[
            pltpu.VMEM((far_count, *mat_shape) if far_count else (1, 16, 128), jnp.bfloat16),
            pltpu.SemaphoreType.DMA((2 * max(1, far_count),)),
        ],
        compiler_params=pltpu.CompilerParams(vmem_limit_bytes=grant(2 * loop_count * mat_bytes)),
        cost_estimate=pl.CostEstimate(
            flops=2 * len(stay) * all_rows * row_count * feat_width,
            bytes_accessed=far_count * mat_bytes,
            transcendentals=0,
        ),
    )(*[mats[m] for m in stay], grad_agg, grad_far, grad_own, w_self)
    pieces = [(message, k) for message, size in zip(arrived, away_groups) for k in range(size)]
    pairs = []
    for term, (message, part) in zip(kept[:-1], pieces):
        pairs += call(
            functools.partial(pair_kernel, part),
            [bf16((row_count, feat_width))],
            [VMEM] * 2 + [pl.BlockSpec(memory_space=pl.ANY)] * len(pairs[-1:]),
            (term, message, *pairs[-1:]),
        )
    back = [swap(pair, "loop", m) for m, pair in zip(far_first, pairs)]
    message, part = pieces[-1]
    (grad_input,) = call(
        functools.partial(sum_kernel, part),
        [bf16((row_count, feat_width))],
        [VMEM] * (2 + len(back)),
        (kept[-1], message, *back),
        flops=0,
    )
    mask = loop_count // 2
    while mask:
        arrived_w = swap(sent_w, "loop", mask)
        dtype = jnp.bfloat16 if mask > 1 else jnp.float32
        earlier = {loop_count // 2: [], 2: pairs[2:3], 1: [token(back, 12_000_000_000)]}.get(mask, [])
        sent_w = added(sent_w, arrived_w, *earlier, dtype=dtype)
        mask //= 2
    other = swap(sent_w[:feat_width], "rep", 1)
    grad_self, grad_neigh, grad_bias = call(
        finish_kernel,
        [f32((feat_width, hidden)), f32((feat_width, hidden)), f32((1, hidden))],
        [VMEM] * 2,
        (sent_w, other),
    )
    return (output, grad_input, grad_self, grad_neigh, grad_bias[0])


def solution(mesh):
    in_specs = (
        P(("loop", "rep"), None),
        P(),
        P(),
        P(),
        P(("loop", "rep")),
        P("loop", "rep", None, None, None, None),
        P("loop", "rep", None, None),
        P("loop", "rep", None, None),
        P("loop", "rep", None),
        P(("loop", "rep"), None),
    )
    out_specs = (P(("loop", "rep"), None), P(("loop", "rep"), None), P(), P(), P())
    return jax.shard_map(
        per_device, mesh=mesh, in_specs=in_specs, out_specs=out_specs, check_vma=False
    )
```

```python
import functools
import math

import jax
import jax.numpy as jnp
from jax import lax
from jax.experimental import pallas as pl
from jax.experimental.pallas import tpu as pltpu
from jax.sharding import PartitionSpec as P

VMEM = pl.BlockSpec(memory_space=pltpu.VMEM)
HBM = pl.BlockSpec(memory_space=pltpu.HBM)


def swap(block, axis, mask):
    return lax.ppermute(block, axis, [(i, i ^ mask) for i in range(lax.axis_size(axis))])


def grant(held):
    return min(held + (4 << 20), 56 << 20)


def call(kernel, out_shape, in_specs, args, flops=0):
    moved = sum(math.prod(a.shape) * a.dtype.itemsize for a in (*args, *out_shape))
    return pl.pallas_call(
        kernel,
        out_shape=list(out_shape),
        in_specs=in_specs,
        out_specs=[VMEM] * len(out_shape),
        compiler_params=pltpu.CompilerParams(vmem_limit_bytes=grant(moved)),
        cost_estimate=pl.CostEstimate(flops=flops, bytes_accessed=moved, transcendentals=0),
    )(*args)


def after(value, *earlier):
    return lax.optimization_barrier((value, *earlier))


def in_hbm(value):
    return pltpu.with_memory_space_constraint(value, pltpu.HBM)


def f32(shape):
    return jax.ShapeDtypeStruct(shape, jnp.float32)


def bf16(shape):
    return jax.ShapeDtypeStruct(shape, jnp.bfloat16)


def place_kernel(
    near_count, order, rep_count, sub_blocks, packs, dst_far, src_far, live_far, tiles, *refs
):
    count = len(order)
    sides, refs = (refs[:3], refs[3:]) if packs else ((), refs)
    mats, refs = refs[:count], refs[count:]
    if packs:
        bundle, refs = refs[0], refs[1:]
    dst, src, live, stage, degree, read, done, left = refs
    tile_size = tiles.shape[-1]
    loop_here, rep_here = lax.axis_index("loop"), lax.axis_index("rep")
    sub_bits = sub_blocks.bit_length() - 1
    moves = [(dst_far, dst), (src_far, src), (live_far, live)]
    if packs:
        width = sides[0].shape[1]
        moves += [
            (sides[1], degree),
            (sides[0], bundle.at[:, pl.ds(0, width)]),
            (sides[2], bundle.at[:, pl.ds(2 * width, bundle.shape[1] - 2 * width)]),
        ]
    moves = [pltpu.make_async_copy(far, near, read.at[k]) for k, (far, near) in enumerate(moves)]
    for move in moves:
        move.start()
    built = [mats[k] if k < near_count else stage.at[k - near_count] for k in range(count)]

    def copy(k, source, slot, row, column):
        rows = pl.ds(pl.multiple_of(row * tile_size, tile_size), tile_size)
        columns = pl.ds(pl.multiple_of(column * tile_size, tile_size), tile_size)
        return pltpu.make_async_copy(
            tiles.at[source, slot], built[k].at[rows, columns], done.at[k]
        )

    backward = list(reversed(range(count)))
    for k in backward:
        built[k][...] = jnp.zeros(built[k].shape, jnp.bfloat16)
        if k == count - 1:
            for move in moves[:3]:
                move.wait()
        source = loop_here ^ order[k]

        def put(slot, carry):
            block, column = dst[source, slot], src[source, slot]
            away = lax.shift_right_logical(block, sub_bits) ^ rep_here
            panel = (away & 1) * (rep_count // 2) + lax.shift_right_logical(away, 1)
            row = panel * sub_blocks + (block & (sub_blocks - 1))
            copy(k, source, slot, row, column).start()
            return carry

        lax.fori_loop(0, live[0, source], put, 0)
    if packs:
        for move in moves[3:]:
            move.wait()
        degree_f = jnp.broadcast_to(degree[...].astype(jnp.float32), (width, bundle.shape[0]))
        bundle[:, width : 2 * width] = degree_f.T.astype(jnp.bfloat16)
    for k in backward:

        def finish(slot, carry):
            copy(k, 0, 0, 0, 0).wait()
            return carry

        lax.fori_loop(0, live[0, loop_here ^ order[k]], finish, 0)
        if k >= near_count:
            pltpu.make_async_copy(built[k], mats[k], left.at[k - near_count]).start()
    for k in range(near_count, count):
        pltpu.make_async_copy(built[k], mats[k], left.at[k - near_count]).wait()


def fetched(mats, near_count, stage, done):
    fetches = []
    for k, mat in enumerate(mats[near_count:]):
        half = mat.shape[0] // 2
        for part in range(2):
            rows = pl.ds(part * half, half)
            fetches.append(
                pltpu.make_async_copy(mat.at[rows], stage.at[k, rows], done.at[2 * k + part])
            )
    for fetch in fetches:
        fetch.start()

    def take(j):
        if j < near_count:
            return mats[j]
        for fetch in fetches[2 * (j - near_count) : 2 * (j - near_count) + 2]:
            fetch.wait()
        return stage.at[j - near_count]

    return take


def gather_first_kernel(near_count, count, *refs):
    mats, panels, (out, stage, done) = refs[:count], refs[count:-3], refs[-3:]
    take = fetched(mats, near_count, stage, done)
    total_rows = out.shape[0]
    chunk = min(256, total_rows)
    for j, panel in enumerate(panels):
        mat = take(j)
        for at in range(0, total_rows, chunk):
            rows = slice(at, at + chunk)
            term = jnp.dot(mat[rows, :], panel[...], preferred_element_type=jnp.float32)
            out[rows, :] = term if j == 0 else out[rows, :] + term


def gather_more_kernel(mat, panel, so_far, out):
    total_rows = out.shape[0]
    chunk = min(256, total_rows)
    for at in range(0, total_rows, chunk):
        rows = slice(at, at + chunk)
        out[rows, :] = so_far[rows, :] + jnp.dot(
            mat[rows, :], panel[...], preferred_element_type=jnp.float32
        )


def gather_last_kernel(count, *refs):
    mats, panels, (so_far, keep, send) = refs[:count], refs[count : 2 * count], refs[2 * count :]
    half = keep.shape[0]
    chunk = min(256, half)
    for at in range(0, 2 * half, chunk):
        rows = slice(at, at + chunk)
        total = so_far[rows, :]
        for mat, panel in zip(mats, panels):
            total += jnp.dot(mat[rows, :], panel[...], preferred_element_type=jnp.float32)
        if at < half:
            keep[rows, :] = total
        else:
            send[at - half : at - half + chunk, :] = total.astype(jnp.bfloat16)


def add_kernel(kept, arrived, *refs):
    out = refs[-1]
    out[...] = (kept[...].astype(jnp.float32) + arrived[...].astype(jnp.float32)).astype(out.dtype)


def middle_kernel(
    flip, total, term, w_self, w_neigh, bias, *refs
):
    bundles, (output, grad_pre, aggregate, grad_agg) = refs[:-4], refs[-4:]
    row_count, width = bundles[0].shape[0], w_neigh.shape[0]
    for j, bundle in enumerate(bundles):
        rows = slice(j * row_count, (j + 1) * row_count)
        there = slice((j ^ flip) * row_count, ((j ^ flip) + 1) * row_count)
        degree_f = bundle[:, width : width + 1].astype(jnp.float32)
        agg = (
            (total[rows, :].astype(jnp.float32) + term[there, :].astype(jnp.float32)) / degree_f
        ).astype(jnp.bfloat16)
        features = bundle[:, :width]
        preact = (
            jnp.dot(
                jnp.concatenate([features, agg], axis=1),
                jnp.concatenate([w_self[...], w_neigh[...]], axis=0),
                preferred_element_type=jnp.float32,
            )
            + bias[...]
        )
        sigmoid_val = jax.nn.sigmoid(preact)
        grad = (
            bundle[:, 2 * width :].astype(jnp.float32)
            * sigmoid_val
            * (1.0 + preact * (1.0 - sigmoid_val))
        ).astype(jnp.bfloat16)
        if j == 0:
            output[...] = (preact * sigmoid_val).astype(jnp.bfloat16)
        grad_pre[rows, :] = grad
        aggregate[rows, :] = agg
        back = lax.dot_general(
            grad, w_neigh[...], (((1,), (1,)), ((), ())), preferred_element_type=jnp.float32
        )
        grad_agg[rows, :] = (back / degree_f).astype(jnp.bfloat16)


def weight_kernel(scale, aggregate, grad_pre, *refs):
    bundles, (keep, send) = refs[:-2], refs[-2:]
    row_count, width = bundles[0].shape[0], aggregate.shape[1]
    parts = []
    for j, bundle in enumerate(bundles):
        rows = slice(j * row_count, (j + 1) * row_count)
        grad = grad_pre[rows, :]
        grads = [
            lax.dot_general(
                a, grad, (((0,), (0,)), ((), ())), preferred_element_type=jnp.float32
            )
            for a in (bundle[:, :width], aggregate[rows, :])
        ]
        parts.append((*grads, jnp.sum(grad.astype(jnp.float32), axis=0, keepdims=True)))
    while len(parts) > 1:
        parts = [
            tuple(x + y for x, y in zip(a, b)) for a, b in zip(parts[::2], parts[1::2])
        ]
    by_self, by_neigh, by_bias = (p * scale for p in parts[0])
    first = (lax.axis_index("rep") & 1) == 0
    for out, mine in ((keep, first), (send, jnp.logical_not(first))):
        out[:width, :] = jnp.where(mine, by_self, by_neigh)
        out[width:, :] = jnp.broadcast_to(by_bias, (out.shape[0] - width, by_bias.shape[1]))


def spread(mat, near_t, far_t):
    half = near_t.shape[1]
    total = jnp.dot(near_t, mat[:half, :], preferred_element_type=jnp.float32)
    total += jnp.dot(far_t, mat[half:, :], preferred_element_type=jnp.float32)
    return total.T


def spread_near_kernel(count, *refs):
    mats, near, outs = refs[:count], refs[count], refs[count + 1 :]
    near_t = near[...].T
    for mat, out in zip(mats, outs):
        half = near.shape[0]
        out[...] = jnp.dot(near_t, mat[:half, :], preferred_element_type=jnp.float32)


def spread_away_kernel(groups, *refs):
    count = sum(groups)
    mats, begun, far, outs = (
        refs[:count],
        refs[count : 2 * count],
        refs[2 * count],
        refs[2 * count + 1 :],
    )
    far_t = far[...].T
    half = far.shape[0]
    j = 0
    for size, out in zip(groups, outs):
        rows = out.shape[0] // size
        for k in range(size):
            term = begun[j][...] + jnp.dot(
                far_t, mats[j][half:, :], preferred_element_type=jnp.float32
            )
            out[k * rows : (k + 1) * rows, :] = term.T.astype(jnp.bfloat16)
            j += 1


def spread_here_kernel(near_count, count, *refs):
    mats, (near, far, grad_pre, w_self, held) = refs[:count], refs[count : count + 5]
    outs, (output, stage, done, left) = refs[count + 5 : -4], refs[-4:]
    leave = pltpu.make_async_copy(held, output, left)
    leave.start()
    take = fetched(mats, near_count, stage, done)
    near_t, far_t = near[...].T, far[...].T
    for j, out in enumerate(outs):
        term = spread(take(j), near_t, far_t)
        if j == count - 1:
            term += lax.dot_general(
                grad_pre[: out.shape[0], :],
                w_self[...],
                (((1,), (1,)), ((), ())),
                preferred_element_type=jnp.float32,
            )
        out[...] = term.astype(out.dtype)
    leave.wait()


def pair_kernel(part, term, message, *refs):
    out = refs[-1]
    rows = out.shape[0]
    piece = message[part * rows : (part + 1) * rows, :]
    out[...] = (term[...].astype(jnp.float32) + piece.astype(jnp.float32)).astype(out.dtype)


def sum_kernel(part, own, message, *refs):
    arrived, out = refs[:-1], refs[-1]
    rows = out.shape[0]
    total = own[...] + message[part * rows : (part + 1) * rows, :].astype(jnp.float32)
    for term in arrived:
        total += term[...].astype(jnp.float32)
    out[...] = total.astype(out.dtype)


def finish_kernel(weights, other, grad_self, grad_neigh, grad_bias):
    width = grad_self.shape[0]
    first = (lax.axis_index("rep") & 1) == 0
    mine = weights[:width, :]
    grad_self[...] = jnp.where(first, mine, other[...])
    grad_neigh[...] = jnp.where(first, other[...], mine)
    grad_bias[...] = weights[width : width + 1, :]


def token_kernel(*refs):
    refs[-1][...] = jnp.zeros(refs[-1].shape, jnp.float32)


def token(values, flops):
    (out,) = call(
        token_kernel,
        [f32((8, 128))],
        [pl.BlockSpec(memory_space=pl.ANY)] * len(values),
        values,
        flops=flops,
    )
    return out


def added(kept, arrived, *earlier, dtype=jnp.bfloat16):
    (total,) = call(
        add_kernel,
        [jax.ShapeDtypeStruct(kept.shape, dtype)],
        [VMEM] * 2 + [pl.BlockSpec(memory_space=pl.ANY)] * len(earlier),
        (kept, arrived, *earlier),
    )
    return total


def per_device(
    features, w_self, w_neigh, bias, degree, tiles, dst_block, src_block, live_count, cotangent
):
    loop_count = lax.axis_size("loop")
    rep_count = lax.axis_size("rep")
    row_count, feat_width = features.shape
    hidden = w_self.shape[1]
    tile_size = tiles.shape[-1]
    sub_blocks = row_count // tile_size
    all_rows = row_count * rep_count
    half_rows = all_rows // 2

    far_first = list(range(loop_count - 2, 0, -2))
    panels = {0: features}
    for mask in (*far_first, 1):
        panels[mask] = swap(features, "loop", mask)

    mat_shape = (all_rows, row_count)
    mat_bytes = 2 * all_rows * row_count
    small = loop_count * mat_bytes <= 8 << 20
    late = [m ^ 1 for m in far_first]
    stay = [*far_first, 0]
    far_count = 0 if small else len(stay)
    graph = (dst_block[0, 0], src_block[0, 0], live_count[0], tiles[0, 0])
    sides = (features, degree[None, :], cotangent)

    def place(masks, far, packs):
        near_count = 0 if far else len(masks)
        kind = pltpu.HBM if far else jax.ShapeDtypeStruct
        bundle = [bf16((row_count, 2 * feat_width + hidden))] if packs else []
        operands = graph + sides if packs else graph
        placed = pl.pallas_call(
            functools.partial(place_kernel, near_count, masks, rep_count, sub_blocks, packs),
            out_shape=[kind(mat_shape, jnp.bfloat16)] * len(masks) + bundle,
            in_specs=[HBM] * len(operands),
            out_specs=[HBM if far else VMEM] * len(masks) + [VMEM] * len(bundle),
            scratch_shapes=[pltpu.SMEM(g.shape, jnp.int32) for g in graph[:3]]
            + [
                pltpu.VMEM((len(masks), *mat_shape) if far else (1, 16, 128), jnp.bfloat16),
                pltpu.VMEM((1, row_count), jnp.int32),
                pltpu.SemaphoreType.DMA((6,)),
                pltpu.SemaphoreType.DMA((len(masks),)),
                pltpu.SemaphoreType.DMA((len(masks),)),
            ],
            compiler_params=pltpu.CompilerParams(vmem_limit_bytes=grant(len(masks) * mat_bytes)),
            cost_estimate=pl.CostEstimate(
                flops=0, bytes_accessed=2 * len(masks) * mat_bytes, transcendentals=0
            ),
        )(*map(in_hbm, operands))
        mats = [in_hbm(mat) if far else mat for mat in placed[: len(masks)]]
        return dict(zip(masks, mats)), placed[len(masks) :]

    away_masks = [*late, 1]
    mats, (bundle,) = place(away_masks + stay if small else away_masks, False, True)
    if not small:
        mats |= place(stay, True, False)[0]
    bundles = [bundle] + [swap(bundle, "rep", mask) for mask in range(2, rep_count, 2)]
    arrivals = [*far_first[:0:-1], far_first[0], 1]
    mats[late[0]], *got = after(mats[late[0]], *[panels[m] for m in arrivals])
    panels.update(zip(arrivals, got))
    for mask in arrivals[:-1]:
        panels[mask ^ 1] = swap(panels[mask], "loop", 1)

    early = [1, *stay]
    (running,) = pl.pallas_call(
        functools.partial(gather_first_kernel, len(early) - far_count, len(early)),
        out_shape=[f32((all_rows, feat_width))],
        in_specs=[VMEM] * (len(early) - far_count)
        + [HBM] * far_count
        + [VMEM] * len(early),
        out_specs=[VMEM],
        scratch_shapes=[
            pltpu.VMEM((far_count, *mat_shape) if far_count else (1, 16, 128), jnp.bfloat16),
            pltpu.SemaphoreType.DMA((2 * max(1, far_count),)),
        ],
        compiler_params=pltpu.CompilerParams(vmem_limit_bytes=grant(2 * loop_count * mat_bytes)),
        cost_estimate=pl.CostEstimate(
            flops=2 * len(early) * all_rows * row_count * feat_width,
            bytes_accessed=far_count * mat_bytes,
            transcendentals=0,
        ),
    )(*[mats[m] for m in early], *[panels[m] for m in early])
    *sooner, latest = [m ^ 1 for m in arrivals[:-1]]
    for mask in sooner:
        (running,) = call(
            gather_more_kernel,
            [f32((all_rows, feat_width))],
            [VMEM] * 3,
            (mats[mask], panels[mask], running),
        )
    keep, send = call(
        functools.partial(gather_last_kernel, 1),
        [f32((half_rows, feat_width)), bf16((half_rows, feat_width))],
        [VMEM] * 3,
        (mats[latest], panels[latest], running),
    )
    total = added(keep, swap(send, "rep", 1))
    total, *bundles = after(total, *bundles)
    mask = 2
    while True:
        term = swap(total, "rep", mask)
        if 2 * mask >= rep_count:
            break
        blocks = term.reshape(-1, 2, mask // 2 * row_count, feat_width)[:, ::-1]
        total = (
            total.astype(jnp.float32) + blocks.reshape(half_rows, feat_width).astype(jnp.float32)
        ).astype(jnp.bfloat16)
        mask *= 2

    scale = 1.0 / math.sqrt(row_count * loop_count * rep_count)
    weight_shape = (feat_width + 16, hidden)
    output_shape = (row_count, hidden)
    output, grad_pre, aggregate, grad_agg = call(
        functools.partial(middle_kernel, mask // 2),
        [
            bf16(output_shape),
            bf16((half_rows, hidden)),
            bf16((half_rows, feat_width)),
            bf16((half_rows, feat_width)),
        ],
        [VMEM] * (5 + len(bundles)),
        (total, term, w_self, w_neigh, bias[None, :], *bundles),
        flops=4 * half_rows * feat_width * hidden,
    )
    grad_far = swap(grad_agg, "rep", 1)
    keep_w, send_w = call(
        functools.partial(weight_kernel, scale),
        [f32(weight_shape)] * 2,
        [VMEM] * (2 + len(bundles)),
        (aggregate, grad_pre, *bundles),
        flops=4 * half_rows * feat_width * hidden,
    )
    sent_w = added(keep_w, swap(send_w, "rep", 1))

    away_groups = [1] * (len(far_first) - 1) + [2]
    begun = call(
        functools.partial(spread_near_kernel, len(away_masks)),
        [f32((feat_width, row_count))] * len(away_masks),
        [VMEM] * (len(away_masks) + 1),
        (*[mats[m] for m in away_masks], grad_agg),
        flops=len(stay) * all_rows * row_count * feat_width,
    )
    away = call(
        functools.partial(spread_away_kernel, away_groups),
        [bf16((size * row_count, feat_width)) for size in away_groups],
        [VMEM] * (2 * len(away_masks) + 1),
        (*[mats[m] for m in away_masks], *begun, grad_far),
        flops=len(stay) * all_rows * row_count * feat_width,
    )
    arrived = [swap(message, "loop", 1) for message in away]
    grad_far, *away = after(grad_far, *away)
    kept = pl.pallas_call(
        functools.partial(spread_here_kernel, len(stay) - far_count, len(stay)),
        out_shape=[bf16((row_count, feat_width))] * len(far_first)
        + [f32((row_count, feat_width)), pltpu.HBM(output_shape, jnp.bfloat16)],
        in_specs=[VMEM] * (len(stay) - far_count) + [HBM] * far_count + [VMEM] * 5,
        out_specs=[VMEM] * len(stay) + [HBM],
        scratch_shapes=[
            pltpu.VMEM((far_count, *mat_shape) if far_count else (1, 16, 128), jnp.bfloat16),
            pltpu.SemaphoreType.DMA((2 * max(1, far_count),)),
            pltpu.SemaphoreType.DMA,
        ],
        compiler_params=pltpu.CompilerParams(vmem_limit_bytes=grant(2 * loop_count * mat_bytes)),
        cost_estimate=pl.CostEstimate(
            flops=2 * len(stay) * all_rows * row_count * feat_width,
            bytes_accessed=far_count * mat_bytes,
            transcendentals=0,
        ),
    )(*[mats[m] for m in stay], grad_agg, grad_far, grad_pre, w_self, output)
    *kept, output = kept
    arrived_w = swap(sent_w, "loop", loop_count // 2)
    pieces = [(message, k) for message, size in zip(arrived, away_groups) for k in range(size)]
    pairs = []
    for term, (message, part) in zip(kept[:-1], pieces):
        pairs += call(
            functools.partial(pair_kernel, part),
            [bf16((row_count, feat_width))],
            [VMEM] * 2 + [pl.BlockSpec(memory_space=pl.ANY)] * len(pairs[-1:]),
            (term, message, *pairs[-1:]),
        )
    back = [swap(pair, "loop", m) for m, pair in zip(far_first, pairs)]
    mask = loop_count // 4
    while mask:
        sent_w = added(sent_w, arrived_w, *(pairs[2:3] if mask == 1 else []))
        arrived_w = swap(sent_w, "loop", mask)
        mask //= 2
    sent_w = added(sent_w, arrived_w, token(back, 12_000_000_000), dtype=jnp.float32)
    message, part = pieces[-1]
    (grad_input,) = call(
        functools.partial(sum_kernel, part),
        [bf16((row_count, feat_width))],
        [VMEM] * (2 + len(back)),
        (kept[-1], message, *back),
    )
    other = swap(sent_w[:feat_width], "rep", 1)
    grad_self, grad_neigh, grad_bias = call(
        finish_kernel,
        [f32((feat_width, hidden)), f32((feat_width, hidden)), f32((1, hidden))],
        [VMEM] * 2,
        (sent_w, other),
    )
    return (output, grad_input, grad_self, grad_neigh, grad_bias[0])


def solution(mesh):
    in_specs = (
        P(("loop", "rep"), None),
        P(),
        P(),
        P(),
        P(("loop", "rep")),
        P("loop", "rep", None, None, None, None),
        P("loop", "rep", None, None),
        P("loop", "rep", None, None),
        P("loop", "rep", None),
        P(("loop", "rep"), None),
    )
    out_specs = (P(("loop", "rep"), None), P(("loop", "rep"), None), P(), P(), P())
    return jax.shard_map(
        per_device, mesh=mesh, in_specs=in_specs, out_specs=out_specs, check_vma=False
    )
```

```python
import functools
import math

import jax
import jax.numpy as jnp
from jax import lax
from jax.experimental import pallas as pl
from jax.experimental.pallas import tpu as pltpu
from jax.sharding import PartitionSpec as P

VMEM = pl.BlockSpec(memory_space=pltpu.VMEM)
HBM = pl.BlockSpec(memory_space=pltpu.HBM)


def swap(block, axis, mask):
    return lax.ppermute(block, axis, [(i, i ^ mask) for i in range(lax.axis_size(axis))])


def grant(held):
    return min(held + (4 << 20), 56 << 20)


def call(kernel, out_shape, in_specs, args, flops=0):
    moved = sum(math.prod(a.shape) * a.dtype.itemsize for a in (*args, *out_shape))
    return pl.pallas_call(
        kernel,
        out_shape=list(out_shape),
        in_specs=in_specs,
        out_specs=[VMEM] * len(out_shape),
        compiler_params=pltpu.CompilerParams(vmem_limit_bytes=grant(moved)),
        cost_estimate=pl.CostEstimate(flops=flops, bytes_accessed=moved, transcendentals=0),
    )(*args)


def after(value, *earlier):
    return lax.optimization_barrier((value, *earlier))


def in_hbm(value):
    return pltpu.with_memory_space_constraint(value, pltpu.HBM)


def f32(shape):
    return jax.ShapeDtypeStruct(shape, jnp.float32)


def bf16(shape):
    return jax.ShapeDtypeStruct(shape, jnp.bfloat16)


def place_kernel(
    near_count, order, rep_count, sub_blocks, packs, dst_far, src_far, live_far, tiles, *refs
):
    count = len(order)
    sides, refs = (refs[:3], refs[3:]) if packs else ((), refs)
    mats, refs = refs[:count], refs[count:]
    if packs:
        bundle, refs = refs[0], refs[1:]
    dst, src, live, stage, degree, read, done, left = refs
    tile_size = tiles.shape[-1]
    loop_here, rep_here = lax.axis_index("loop"), lax.axis_index("rep")
    sub_bits = sub_blocks.bit_length() - 1
    moves = [(dst_far, dst), (src_far, src), (live_far, live)]
    if packs:
        width = sides[0].shape[1]
        moves += [
            (sides[1], degree),
            (sides[0], bundle.at[:, pl.ds(0, width)]),
            (sides[2], bundle.at[:, pl.ds(2 * width, bundle.shape[1] - 2 * width)]),
        ]
    moves = [pltpu.make_async_copy(far, near, read.at[k]) for k, (far, near) in enumerate(moves)]
    for move in moves:
        move.start()
    built = [mats[k] if k < near_count else stage.at[k - near_count] for k in range(count)]

    def copy(k, source, slot, row, column):
        rows = pl.ds(pl.multiple_of(row * tile_size, tile_size), tile_size)
        columns = pl.ds(pl.multiple_of(column * tile_size, tile_size), tile_size)
        return pltpu.make_async_copy(
            tiles.at[source, slot], built[k].at[rows, columns], done.at[k]
        )

    backward = list(reversed(range(count)))
    for k in backward:
        built[k][...] = jnp.zeros(built[k].shape, jnp.bfloat16)
        if k == count - 1:
            for move in moves[:3]:
                move.wait()
        source = loop_here ^ order[k]

        def put(slot, carry):
            block, column = dst[source, slot], src[source, slot]
            away = lax.shift_right_logical(block, sub_bits) ^ rep_here
            panel = (away & 1) * (rep_count // 2) + lax.shift_right_logical(away, 1)
            row = panel * sub_blocks + (block & (sub_blocks - 1))
            copy(k, source, slot, row, column).start()
            return carry

        lax.fori_loop(0, live[0, source], put, 0)
    if packs:
        for move in moves[3:]:
            move.wait()
        degree_f = jnp.broadcast_to(degree[...].astype(jnp.float32), (width, bundle.shape[0]))
        bundle[:, width : 2 * width] = degree_f.T.astype(jnp.bfloat16)
    for k in backward:

        def finish(slot, carry):
            copy(k, 0, 0, 0, 0).wait()
            return carry

        lax.fori_loop(0, live[0, loop_here ^ order[k]], finish, 0)
        if k >= near_count:
            pltpu.make_async_copy(built[k], mats[k], left.at[k - near_count]).start()
    for k in range(near_count, count):
        pltpu.make_async_copy(built[k], mats[k], left.at[k - near_count]).wait()


def fetched(mats, near_count, stage, done):
    fetches = []
    for k, mat in enumerate(mats[near_count:]):
        half = mat.shape[0] // 2
        for part in range(2):
            rows = pl.ds(part * half, half)
            fetches.append(
                pltpu.make_async_copy(mat.at[rows], stage.at[k, rows], done.at[2 * k + part])
            )
    for fetch in fetches:
        fetch.start()

    def take(j):
        if j < near_count:
            return mats[j]
        for fetch in fetches[2 * (j - near_count) : 2 * (j - near_count) + 2]:
            fetch.wait()
        return stage.at[j - near_count]

    return take


def gather_first_kernel(near_count, count, *refs):
    mats, panels, (out, stage, done) = refs[:count], refs[count:-3], refs[-3:]
    take = fetched(mats, near_count, stage, done)
    total_rows = out.shape[0]
    chunk = min(256, total_rows)
    for j, panel in enumerate(panels):
        mat = take(j)
        for at in range(0, total_rows, chunk):
            rows = slice(at, at + chunk)
            term = jnp.dot(mat[rows, :], panel[...], preferred_element_type=jnp.float32)
            out[rows, :] = term if j == 0 else out[rows, :] + term


def gather_more_kernel(mat, panel, so_far, out):
    total_rows = out.shape[0]
    chunk = min(256, total_rows)
    for at in range(0, total_rows, chunk):
        rows = slice(at, at + chunk)
        out[rows, :] = so_far[rows, :] + jnp.dot(
            mat[rows, :], panel[...], preferred_element_type=jnp.float32
        )


def gather_last_kernel(count, *refs):
    mats, panels, (so_far, keep, send) = refs[:count], refs[count : 2 * count], refs[2 * count :]
    half = keep.shape[0]
    chunk = min(256, half)
    for at in range(0, 2 * half, chunk):
        rows = slice(at, at + chunk)
        total = so_far[rows, :]
        for mat, panel in zip(mats, panels):
            total += jnp.dot(mat[rows, :], panel[...], preferred_element_type=jnp.float32)
        if at < half:
            keep[rows, :] = total
        else:
            send[at - half : at - half + chunk, :] = total.astype(jnp.bfloat16)


def add_kernel(kept, arrived, *refs):
    out = refs[-1]
    out[...] = (kept[...].astype(jnp.float32) + arrived[...].astype(jnp.float32)).astype(out.dtype)


def middle_kernel(
    flip, total, term, w_self, w_neigh, bias, *refs
):
    bundles, (output, grad_pre, aggregate, grad_agg) = refs[:-4], refs[-4:]
    row_count, width = bundles[0].shape[0], w_neigh.shape[0]
    for j, bundle in enumerate(bundles):
        rows = slice(j * row_count, (j + 1) * row_count)
        there = slice((j ^ flip) * row_count, ((j ^ flip) + 1) * row_count)
        degree_f = bundle[:, width : width + 1].astype(jnp.float32)
        agg = (
            (total[rows, :].astype(jnp.float32) + term[there, :].astype(jnp.float32)) / degree_f
        ).astype(jnp.bfloat16)
        features = bundle[:, :width]
        preact = (
            jnp.dot(
                jnp.concatenate([features, agg], axis=1),
                jnp.concatenate([w_self[...], w_neigh[...]], axis=0),
                preferred_element_type=jnp.float32,
            )
            + bias[...]
        )
        sigmoid_val = jax.nn.sigmoid(preact)
        grad = (
            bundle[:, 2 * width :].astype(jnp.float32)
            * sigmoid_val
            * (1.0 + preact * (1.0 - sigmoid_val))
        ).astype(jnp.bfloat16)
        if j == 0:
            output[...] = (preact * sigmoid_val).astype(jnp.bfloat16)
        grad_pre[rows, :] = grad
        aggregate[rows, :] = agg
        back = lax.dot_general(
            grad, w_neigh[...], (((1,), (1,)), ((), ())), preferred_element_type=jnp.float32
        )
        grad_agg[rows, :] = (back / degree_f).astype(jnp.bfloat16)


def weight_kernel(scale, aggregate, grad_pre, *refs):
    bundles, (keep, send) = refs[:-2], refs[-2:]
    row_count, width = bundles[0].shape[0], aggregate.shape[1]
    parts = []
    for j, bundle in enumerate(bundles):
        rows = slice(j * row_count, (j + 1) * row_count)
        grad = grad_pre[rows, :]
        grads = [
            lax.dot_general(
                a, grad, (((0,), (0,)), ((), ())), preferred_element_type=jnp.float32
            )
            for a in (bundle[:, :width], aggregate[rows, :])
        ]
        parts.append((*grads, jnp.sum(grad.astype(jnp.float32), axis=0, keepdims=True)))
    while len(parts) > 1:
        parts = [
            tuple(x + y for x, y in zip(a, b)) for a, b in zip(parts[::2], parts[1::2])
        ]
    by_self, by_neigh, by_bias = (p * scale for p in parts[0])
    first = (lax.axis_index("rep") & 1) == 0
    for out, mine in ((keep, first), (send, jnp.logical_not(first))):
        out[:width, :] = jnp.where(mine, by_self, by_neigh)
        out[width:, :] = jnp.broadcast_to(by_bias, (out.shape[0] - width, by_bias.shape[1]))


def spread(mat, near_t, far_t):
    half = near_t.shape[1]
    total = jnp.dot(near_t, mat[:half, :], preferred_element_type=jnp.float32)
    total += jnp.dot(far_t, mat[half:, :], preferred_element_type=jnp.float32)
    return total.T


def spread_near_kernel(count, *refs):
    mats, near, outs = refs[:count], refs[count], refs[count + 1 :]
    near_t = near[...].T
    for mat, out in zip(mats, outs):
        half = near.shape[0]
        out[...] = jnp.dot(near_t, mat[:half, :], preferred_element_type=jnp.float32)


def spread_away_kernel(groups, *refs):
    count = sum(groups)
    mats, begun, far, outs = (
        refs[:count],
        refs[count : 2 * count],
        refs[2 * count],
        refs[2 * count + 1 :],
    )
    far_t = far[...].T
    half = far.shape[0]
    j = 0
    for size, out in zip(groups, outs):
        rows = out.shape[0] // size
        for k in range(size):
            term = begun[j][...] + jnp.dot(
                far_t, mats[j][half:, :], preferred_element_type=jnp.float32
            )
            out[k * rows : (k + 1) * rows, :] = term.T.astype(jnp.bfloat16)
            j += 1


def spread_here_kernel(near_count, count, *refs):
    mats, (near, far, grad_pre, w_self, held) = refs[:count], refs[count : count + 5]
    outs, (output, stage, done, left) = refs[count + 5 : -4], refs[-4:]
    leave = pltpu.make_async_copy(held, output, left)
    leave.start()
    take = fetched(mats, near_count, stage, done)
    near_t, far_t = near[...].T, far[...].T
    for j, out in enumerate(outs):
        term = spread(take(j), near_t, far_t)
        if j == count - 1:
            term += lax.dot_general(
                grad_pre[: out.shape[0], :],
                w_self[...],
                (((1,), (1,)), ((), ())),
                preferred_element_type=jnp.float32,
            )
        out[...] = term.astype(out.dtype)
    leave.wait()


def pair_kernel(part, term, message, *refs):
    out = refs[-1]
    rows = out.shape[0]
    piece = message[part * rows : (part + 1) * rows, :]
    out[...] = (term[...].astype(jnp.float32) + piece.astype(jnp.float32)).astype(out.dtype)


def sum_kernel(part, own, message, *refs):
    arrived, out = refs[:-1], refs[-1]
    rows = out.shape[0]
    total = own[...] + message[part * rows : (part + 1) * rows, :].astype(jnp.float32)
    for term in arrived:
        total += term[...].astype(jnp.float32)
    out[...] = total.astype(out.dtype)


def finish_kernel(weights, other, grad_self, grad_neigh, grad_bias):
    width = grad_self.shape[0]
    first = (lax.axis_index("rep") & 1) == 0
    mine = weights[:width, :]
    grad_self[...] = jnp.where(first, mine, other[...])
    grad_neigh[...] = jnp.where(first, other[...], mine)
    grad_bias[...] = weights[width : width + 1, :]


def token_kernel(*refs):
    refs[-1][...] = jnp.zeros(refs[-1].shape, jnp.float32)


def token(values, flops):
    (out,) = call(
        token_kernel,
        [f32((8, 128))],
        [pl.BlockSpec(memory_space=pl.ANY)] * len(values),
        values,
        flops=flops,
    )
    return out


def added(kept, arrived, *earlier, dtype=jnp.bfloat16):
    (total,) = call(
        add_kernel,
        [jax.ShapeDtypeStruct(kept.shape, dtype)],
        [VMEM] * 2 + [pl.BlockSpec(memory_space=pl.ANY)] * len(earlier),
        (kept, arrived, *earlier),
    )
    return total


def per_device(
    features, w_self, w_neigh, bias, degree, tiles, dst_block, src_block, live_count, cotangent
):
    loop_count = lax.axis_size("loop")
    rep_count = lax.axis_size("rep")
    row_count, feat_width = features.shape
    hidden = w_self.shape[1]
    tile_size = tiles.shape[-1]
    sub_blocks = row_count // tile_size
    all_rows = row_count * rep_count
    half_rows = all_rows // 2

    far_first = list(range(loop_count - 2, 0, -2))
    panels = {0: features}
    for mask in (*far_first, 1):
        panels[mask] = swap(features, "loop", mask)

    mat_shape = (all_rows, row_count)
    mat_bytes = 2 * all_rows * row_count
    small = loop_count * mat_bytes <= 8 << 20
    late = [m ^ 1 for m in far_first]
    stay = [*far_first, 0]
    far_count = 0 if small else len(stay)
    graph = (dst_block[0, 0], src_block[0, 0], live_count[0], tiles[0, 0])
    sides = (features, degree[None, :], cotangent)

    def place(masks, far, packs):
        near_count = 0 if far else len(masks)
        kind = pltpu.HBM if far else jax.ShapeDtypeStruct
        bundle = [bf16((row_count, 2 * feat_width + hidden))] if packs else []
        operands = graph + sides if packs else graph
        placed = pl.pallas_call(
            functools.partial(place_kernel, near_count, masks, rep_count, sub_blocks, packs),
            out_shape=[kind(mat_shape, jnp.bfloat16)] * len(masks) + bundle,
            in_specs=[HBM] * len(operands),
            out_specs=[HBM if far else VMEM] * len(masks) + [VMEM] * len(bundle),
            scratch_shapes=[pltpu.SMEM(g.shape, jnp.int32) for g in graph[:3]]
            + [
                pltpu.VMEM((len(masks), *mat_shape) if far else (1, 16, 128), jnp.bfloat16),
                pltpu.VMEM((1, row_count), jnp.int32),
                pltpu.SemaphoreType.DMA((6,)),
                pltpu.SemaphoreType.DMA((len(masks),)),
                pltpu.SemaphoreType.DMA((len(masks),)),
            ],
            compiler_params=pltpu.CompilerParams(vmem_limit_bytes=grant(len(masks) * mat_bytes)),
            cost_estimate=pl.CostEstimate(
                flops=0, bytes_accessed=2 * len(masks) * mat_bytes, transcendentals=0
            ),
        )(*map(in_hbm, operands))
        mats = [in_hbm(mat) if far else mat for mat in placed[: len(masks)]]
        return dict(zip(masks, mats)), placed[len(masks) :]

    away_masks = [*late, 1]
    mats, (bundle,) = place(away_masks + stay if small else away_masks, False, True)
    if not small:
        mats |= place(stay, True, False)[0]
    bundles = [bundle] + [swap(bundle, "rep", mask) for mask in range(2, rep_count, 2)]
    arrivals = [*far_first[:0:-1], far_first[0], 1]
    mats[late[0]], *got = after(mats[late[0]], *[panels[m] for m in arrivals])
    panels.update(zip(arrivals, got))
    for mask in arrivals[:-1]:
        panels[mask ^ 1] = swap(panels[mask], "loop", 1)

    early = [1, *stay]
    (running,) = pl.pallas_call(
        functools.partial(gather_first_kernel, len(early) - far_count, len(early)),
        out_shape=[f32((all_rows, feat_width))],
        in_specs=[VMEM] * (len(early) - far_count)
        + [HBM] * far_count
        + [VMEM] * len(early),
        out_specs=[VMEM],
        scratch_shapes=[
            pltpu.VMEM((far_count, *mat_shape) if far_count else (1, 16, 128), jnp.bfloat16),
            pltpu.SemaphoreType.DMA((2 * max(1, far_count),)),
        ],
        compiler_params=pltpu.CompilerParams(vmem_limit_bytes=grant(2 * loop_count * mat_bytes)),
        cost_estimate=pl.CostEstimate(
            flops=2 * len(early) * all_rows * row_count * feat_width,
            bytes_accessed=far_count * mat_bytes,
            transcendentals=0,
        ),
    )(*[mats[m] for m in early], *[panels[m] for m in early])
    *sooner, latest = [m ^ 1 for m in arrivals[:-1]]
    for mask in sooner:
        (running,) = call(
            gather_more_kernel,
            [f32((all_rows, feat_width))],
            [VMEM] * 3,
            (mats[mask], panels[mask], running),
        )
    keep, send = call(
        functools.partial(gather_last_kernel, 1),
        [f32((half_rows, feat_width)), bf16((half_rows, feat_width))],
        [VMEM] * 3,
        (mats[latest], panels[latest], running),
    )
    total = added(keep, swap(send, "rep", 1))
    total, *bundles = after(total, *bundles)
    mask = 2
    while True:
        term = swap(total, "rep", mask)
        if 2 * mask >= rep_count:
            break
        blocks = term.reshape(-1, 2, mask // 2 * row_count, feat_width)[:, ::-1]
        total = (
            total.astype(jnp.float32) + blocks.reshape(half_rows, feat_width).astype(jnp.float32)
        ).astype(jnp.bfloat16)
        mask *= 2

    scale = 1.0 / math.sqrt(row_count * loop_count * rep_count)
    weight_shape = (feat_width + 16, hidden)
    output_shape = (row_count, hidden)
    output, grad_pre, aggregate, grad_agg = call(
        functools.partial(middle_kernel, mask // 2),
        [
            bf16(output_shape),
            bf16((half_rows, hidden)),
            bf16((half_rows, feat_width)),
            bf16((half_rows, feat_width)),
        ],
        [VMEM] * (5 + len(bundles)),
        (total, term, w_self, w_neigh, bias[None, :], *bundles),
        flops=4 * half_rows * feat_width * hidden,
    )
    grad_far = swap(grad_agg, "rep", 1)
    keep_w, send_w = call(
        functools.partial(weight_kernel, scale),
        [f32(weight_shape)] * 2,
        [VMEM] * (2 + len(bundles)),
        (aggregate, grad_pre, *bundles),
        flops=4 * half_rows * feat_width * hidden,
    )
    sent_w = added(keep_w, swap(send_w, "rep", 1))

    away_groups = [1] * (len(far_first) - 1) + [2]
    begun = call(
        functools.partial(spread_near_kernel, len(away_masks)),
        [f32((feat_width, row_count))] * len(away_masks),
        [VMEM] * (len(away_masks) + 1),
        (*[mats[m] for m in away_masks], grad_agg),
        flops=len(stay) * all_rows * row_count * feat_width,
    )
    away = call(
        functools.partial(spread_away_kernel, away_groups),
        [bf16((size * row_count, feat_width)) for size in away_groups],
        [VMEM] * (2 * len(away_masks) + 1),
        (*[mats[m] for m in away_masks], *begun, grad_far),
        flops=len(stay) * all_rows * row_count * feat_width,
    )
    arrived = [swap(message, "loop", 1) for message in away]
    grad_far, *away = after(grad_far, *away)
    kept = pl.pallas_call(
        functools.partial(spread_here_kernel, len(stay) - far_count, len(stay)),
        out_shape=[bf16((row_count, feat_width))] * len(far_first)
        + [f32((row_count, feat_width)), pltpu.HBM(output_shape, jnp.bfloat16)],
        in_specs=[VMEM] * (len(stay) - far_count) + [HBM] * far_count + [VMEM] * 5,
        out_specs=[VMEM] * len(stay) + [HBM],
        scratch_shapes=[
            pltpu.VMEM((far_count, *mat_shape) if far_count else (1, 16, 128), jnp.bfloat16),
            pltpu.SemaphoreType.DMA((2 * max(1, far_count),)),
            pltpu.SemaphoreType.DMA,
        ],
        compiler_params=pltpu.CompilerParams(vmem_limit_bytes=grant(2 * loop_count * mat_bytes)),
        cost_estimate=pl.CostEstimate(
            flops=2 * len(stay) * all_rows * row_count * feat_width,
            bytes_accessed=far_count * mat_bytes,
            transcendentals=0,
        ),
    )(*[mats[m] for m in stay], grad_agg, grad_far, grad_pre, w_self, output)
    *kept, output = kept
    arrived_w = swap(sent_w, "loop", loop_count // 2)
    pieces = [(message, k) for message, size in zip(arrived, away_groups) for k in range(size)]
    pairs = []
    for term, (message, part) in zip(kept[:-1], pieces):
        pairs += call(
            functools.partial(pair_kernel, part),
            [bf16((row_count, feat_width))],
            [VMEM] * 2 + [pl.BlockSpec(memory_space=pl.ANY)] * len(pairs[-1:]),
            (term, message, *pairs[-1:]),
        )
    back = [swap(pair, "loop", m) for m, pair in zip(far_first, pairs)]
    mask = loop_count // 4
    while mask:
        sent_w = added(sent_w, arrived_w, *(pairs[2:3] if mask == 1 else kept[:1]))
        arrived_w = swap(sent_w, "loop", mask)
        mask //= 2
    sent_w = added(sent_w, arrived_w, token(back, 12_000_000_000), dtype=jnp.float32)
    message, part = pieces[-1]
    (grad_input,) = call(
        functools.partial(sum_kernel, part),
        [bf16((row_count, feat_width))],
        [VMEM] * (2 + len(back)),
        (kept[-1], message, *back),
    )
    other = swap(sent_w[:feat_width], "rep", 1)
    grad_self, grad_neigh, grad_bias = call(
        finish_kernel,
        [f32((feat_width, hidden)), f32((feat_width, hidden)), f32((1, hidden))],
        [VMEM] * 2,
        (sent_w, other),
    )
    return (output, grad_input, grad_self, grad_neigh, grad_bias[0])


def solution(mesh):
    in_specs = (
        P(("loop", "rep"), None),
        P(),
        P(),
        P(),
        P(("loop", "rep")),
        P("loop", "rep", None, None, None, None),
        P("loop", "rep", None, None),
        P("loop", "rep", None, None),
        P("loop", "rep", None),
        P(("loop", "rep"), None),
    )
    out_specs = (P(("loop", "rep"), None), P(("loop", "rep"), None), P(), P(), P())
    return jax.shard_map(
        per_device, mesh=mesh, in_specs=in_specs, out_specs=out_specs, check_vma=False
    )
```

```python
import functools
import math

import jax
import jax.numpy as jnp
from jax import lax
from jax.experimental import pallas as pl
from jax.experimental.pallas import tpu as pltpu
from jax.sharding import PartitionSpec as P

VMEM = pl.BlockSpec(memory_space=pltpu.VMEM)
HBM = pl.BlockSpec(memory_space=pltpu.HBM)


def swap(block, axis, mask):
    return lax.ppermute(block, axis, [(i, i ^ mask) for i in range(lax.axis_size(axis))])


def grant(held):
    return min(held + (4 << 20), 56 << 20)


def call(kernel, out_shape, in_specs, args, flops=0):
    moved = sum(math.prod(a.shape) * a.dtype.itemsize for a in (*args, *out_shape))
    return pl.pallas_call(
        kernel,
        out_shape=list(out_shape),
        in_specs=in_specs,
        out_specs=[VMEM] * len(out_shape),
        compiler_params=pltpu.CompilerParams(vmem_limit_bytes=grant(moved)),
        cost_estimate=pl.CostEstimate(flops=flops, bytes_accessed=moved, transcendentals=0),
    )(*args)


def after(value, *earlier):
    return lax.optimization_barrier((value, *earlier))


def in_hbm(value):
    return pltpu.with_memory_space_constraint(value, pltpu.HBM)


def f32(shape):
    return jax.ShapeDtypeStruct(shape, jnp.float32)


def bf16(shape):
    return jax.ShapeDtypeStruct(shape, jnp.bfloat16)


def place_kernel(
    near_count, order, rep_count, sub_blocks, packs, dst_far, src_far, live_far, tiles, *refs
):
    count = len(order)
    sides, refs = (refs[:3], refs[3:]) if packs else ((), refs)
    mats, refs = refs[:count], refs[count:]
    if packs:
        bundle, refs = refs[0], refs[1:]
    dst, src, live, stage, degree, read, done, left = refs
    tile_size = tiles.shape[-1]
    loop_here, rep_here = lax.axis_index("loop"), lax.axis_index("rep")
    sub_bits = sub_blocks.bit_length() - 1
    moves = [(dst_far, dst), (src_far, src), (live_far, live)]
    if packs:
        rows, width = sides[0].shape
        moves += [
            (sides[1], degree),
            (sides[0], bundle.at[pl.ds(0, rows), pl.ds(0, width)]),
            (sides[2], bundle.at[pl.ds(0, rows), pl.ds(width, bundle.shape[1] - width)]),
        ]
    moves = [pltpu.make_async_copy(far, near, read.at[k]) for k, (far, near) in enumerate(moves)]
    for move in moves:
        move.start()
    built = [mats[k] if k < near_count else stage.at[k - near_count] for k in range(count)]

    def copy(k, source, slot, row, column):
        rows = pl.ds(pl.multiple_of(row * tile_size, tile_size), tile_size)
        columns = pl.ds(pl.multiple_of(column * tile_size, tile_size), tile_size)
        return pltpu.make_async_copy(
            tiles.at[source, slot], built[k].at[rows, columns], done.at[k]
        )

    backward = list(reversed(range(count)))
    for k in backward:
        built[k][...] = jnp.zeros(built[k].shape, jnp.bfloat16)
        if k == count - 1:
            for move in moves[:3]:
                move.wait()
        source = loop_here ^ order[k]

        def put(slot, carry):
            block, column = dst[source, slot], src[source, slot]
            away = lax.shift_right_logical(block, sub_bits) ^ rep_here
            panel = (away & 1) * (rep_count // 2) + lax.shift_right_logical(away, 1)
            row = panel * sub_blocks + (block & (sub_blocks - 1))
            copy(k, source, slot, row, column).start()
            return carry

        lax.fori_loop(0, live[0, source], put, 0)
    if packs:
        for move in moves[3:]:
            move.wait()
        degree_rows = jnp.broadcast_to(degree[...].astype(jnp.float32), (16, rows))
        bundle[rows:, :rows] = degree_rows.astype(jnp.bfloat16)
    for k in backward:

        def finish(slot, carry):
            copy(k, 0, 0, 0, 0).wait()
            return carry

        lax.fori_loop(0, live[0, loop_here ^ order[k]], finish, 0)
        if k >= near_count:
            pltpu.make_async_copy(built[k], mats[k], left.at[k - near_count]).start()
    for k in range(near_count, count):
        pltpu.make_async_copy(built[k], mats[k], left.at[k - near_count]).wait()


def fetched(mats, near_count, stage, done):
    fetches = []
    for k, mat in enumerate(mats[near_count:]):
        half = mat.shape[0] // 2
        for part in range(2):
            rows = pl.ds(part * half, half)
            fetches.append(
                pltpu.make_async_copy(mat.at[rows], stage.at[k, rows], done.at[2 * k + part])
            )
    for fetch in fetches:
        fetch.start()

    def take(j):
        if j < near_count:
            return mats[j]
        for fetch in fetches[2 * (j - near_count) : 2 * (j - near_count) + 2]:
            fetch.wait()
        return stage.at[j - near_count]

    return take


def gather_first_kernel(near_count, count, *refs):
    mats, panels, (out, stage, done) = refs[:count], refs[count:-3], refs[-3:]
    take = fetched(mats, near_count, stage, done)
    total_rows = out.shape[0]
    chunk = min(256, total_rows)
    for j, panel in enumerate(panels):
        mat = take(j)
        for at in range(0, total_rows, chunk):
            rows = slice(at, at + chunk)
            term = jnp.dot(mat[rows, :], panel[...], preferred_element_type=jnp.float32)
            out[rows, :] = term if j == 0 else out[rows, :] + term


def gather_more_kernel(mat, panel, so_far, out):
    total_rows = out.shape[0]
    chunk = min(256, total_rows)
    for at in range(0, total_rows, chunk):
        rows = slice(at, at + chunk)
        out[rows, :] = so_far[rows, :] + jnp.dot(
            mat[rows, :], panel[...], preferred_element_type=jnp.float32
        )


def gather_last_kernel(count, *refs):
    mats, panels, (so_far, keep, send) = refs[:count], refs[count : 2 * count], refs[2 * count :]
    half = keep.shape[0]
    chunk = min(256, half)
    for at in range(0, 2 * half, chunk):
        rows = slice(at, at + chunk)
        total = so_far[rows, :]
        for mat, panel in zip(mats, panels):
            total += jnp.dot(mat[rows, :], panel[...], preferred_element_type=jnp.float32)
        if at < half:
            keep[rows, :] = total
        else:
            send[at - half : at - half + chunk, :] = total.astype(jnp.bfloat16)


def add_kernel(kept, arrived, *refs):
    out = refs[-1]
    out[...] = (kept[...].astype(jnp.float32) + arrived[...].astype(jnp.float32)).astype(out.dtype)


def middle_kernel(
    flip, total, term, w_self, w_neigh, bias, *refs
):
    bundles, (output, grad_pre, aggregate, grad_agg) = refs[:-4], refs[-4:]
    row_count, width = bundles[0].shape[0] - 16, w_neigh.shape[0]
    for j, bundle in enumerate(bundles):
        rows = slice(j * row_count, (j + 1) * row_count)
        there = slice((j ^ flip) * row_count, ((j ^ flip) + 1) * row_count)
        degree_row = bundle[row_count : row_count + 1, :row_count].astype(jnp.float32)
        degree_f = jnp.broadcast_to(degree_row, (width, row_count)).T[:, :1]
        agg = (
            (total[rows, :].astype(jnp.float32) + term[there, :].astype(jnp.float32)) / degree_f
        ).astype(jnp.bfloat16)
        features = bundle[:row_count, :width]
        preact = (
            jnp.dot(
                jnp.concatenate([features, agg], axis=1),
                jnp.concatenate([w_self[...], w_neigh[...]], axis=0),
                preferred_element_type=jnp.float32,
            )
            + bias[...]
        )
        sigmoid_val = jax.nn.sigmoid(preact)
        grad = (
            bundle[:row_count, width:].astype(jnp.float32)
            * sigmoid_val
            * (1.0 + preact * (1.0 - sigmoid_val))
        ).astype(jnp.bfloat16)
        if j == 0:
            output[...] = (preact * sigmoid_val).astype(jnp.bfloat16)
        grad_pre[rows, :] = grad
        aggregate[rows, :] = agg
        back = lax.dot_general(
            grad, w_neigh[...], (((1,), (1,)), ((), ())), preferred_element_type=jnp.float32
        )
        grad_agg[rows, :] = (back / degree_f).astype(jnp.bfloat16)


def weight_kernel(scale, aggregate, grad_pre, *refs):
    bundles, (keep, send) = refs[:-2], refs[-2:]
    row_count, width = bundles[0].shape[0] - 16, aggregate.shape[1]
    parts = []
    for j, bundle in enumerate(bundles):
        rows = slice(j * row_count, (j + 1) * row_count)
        grad = grad_pre[rows, :]
        grads = [
            lax.dot_general(
                a, grad, (((0,), (0,)), ((), ())), preferred_element_type=jnp.float32
            )
            for a in (bundle[:row_count, :width], aggregate[rows, :])
        ]
        parts.append((*grads, jnp.sum(grad.astype(jnp.float32), axis=0, keepdims=True)))
    while len(parts) > 1:
        parts = [
            tuple(x + y for x, y in zip(a, b)) for a, b in zip(parts[::2], parts[1::2])
        ]
    by_self, by_neigh, by_bias = (p * scale for p in parts[0])
    first = (lax.axis_index("rep") & 1) == 0
    for out, mine in ((keep, first), (send, jnp.logical_not(first))):
        out[:width, :] = jnp.where(mine, by_self, by_neigh)
        out[width:, :] = jnp.broadcast_to(by_bias, (out.shape[0] - width, by_bias.shape[1]))


def spread(mat, near_t, far_t):
    half = near_t.shape[1]
    total = jnp.dot(near_t, mat[:half, :], preferred_element_type=jnp.float32)
    total += jnp.dot(far_t, mat[half:, :], preferred_element_type=jnp.float32)
    return total.T


def spread_near_kernel(count, *refs):
    mats, near, outs = refs[:count], refs[count], refs[count + 1 :]
    near_t = near[...].T
    for mat, out in zip(mats, outs):
        half = near.shape[0]
        out[...] = jnp.dot(near_t, mat[:half, :], preferred_element_type=jnp.float32)


def spread_away_kernel(groups, *refs):
    count = sum(groups)
    mats, begun, far, outs = (
        refs[:count],
        refs[count : 2 * count],
        refs[2 * count],
        refs[2 * count + 1 :],
    )
    far_t = far[...].T
    half = far.shape[0]
    j = 0
    for size, out in zip(groups, outs):
        rows = out.shape[0] // size
        for k in range(size):
            term = begun[j][...] + jnp.dot(
                far_t, mats[j][half:, :], preferred_element_type=jnp.float32
            )
            out[k * rows : (k + 1) * rows, :] = term.T.astype(jnp.bfloat16)
            j += 1


def spread_here_kernel(near_count, count, *refs):
    mats, (near, far, grad_pre, w_self, held) = refs[:count], refs[count : count + 5]
    outs, (output, stage, done, left) = refs[count + 5 : -4], refs[-4:]
    leave = pltpu.make_async_copy(held, output, left)
    leave.start()
    take = fetched(mats, near_count, stage, done)
    near_t, far_t = near[...].T, far[...].T
    for j, out in enumerate(outs):
        term = spread(take(j), near_t, far_t)
        if j == count - 1:
            term += lax.dot_general(
                grad_pre[: out.shape[0], :],
                w_self[...],
                (((1,), (1,)), ((), ())),
                preferred_element_type=jnp.float32,
            )
        out[...] = term.astype(out.dtype)
    leave.wait()


def pair_kernel(part, term, message, *refs):
    out = refs[-1]
    rows = out.shape[0]
    piece = message[part * rows : (part + 1) * rows, :]
    out[...] = (term[...].astype(jnp.float32) + piece.astype(jnp.float32)).astype(out.dtype)


def sum_kernel(part, own, message, *refs):
    arrived, out = refs[:-1], refs[-1]
    rows = out.shape[0]
    total = own[...] + message[part * rows : (part + 1) * rows, :].astype(jnp.float32)
    for term in arrived:
        total += term[...].astype(jnp.float32)
    out[...] = total.astype(out.dtype)


def finish_kernel(weights, other, grad_self, grad_neigh, grad_bias):
    width = grad_self.shape[0]
    first = (lax.axis_index("rep") & 1) == 0
    mine = weights[:width, :]
    grad_self[...] = jnp.where(first, mine, other[...])
    grad_neigh[...] = jnp.where(first, other[...], mine)
    grad_bias[...] = weights[width : width + 1, :]


def token_kernel(*refs):
    refs[-1][...] = jnp.zeros(refs[-1].shape, jnp.float32)


def token(values, flops):
    (out,) = call(
        token_kernel,
        [f32((8, 128))],
        [pl.BlockSpec(memory_space=pl.ANY)] * len(values),
        values,
        flops=flops,
    )
    return out


def added(kept, arrived, *earlier, dtype=jnp.bfloat16):
    (total,) = call(
        add_kernel,
        [jax.ShapeDtypeStruct(kept.shape, dtype)],
        [VMEM] * 2 + [pl.BlockSpec(memory_space=pl.ANY)] * len(earlier),
        (kept, arrived, *earlier),
    )
    return total


def per_device(
    features, w_self, w_neigh, bias, degree, tiles, dst_block, src_block, live_count, cotangent
):
    loop_count = lax.axis_size("loop")
    rep_count = lax.axis_size("rep")
    row_count, feat_width = features.shape
    hidden = w_self.shape[1]
    tile_size = tiles.shape[-1]
    sub_blocks = row_count // tile_size
    all_rows = row_count * rep_count
    half_rows = all_rows // 2

    far_first = list(range(loop_count - 2, 0, -2))
    panels = {0: features}
    for mask in (*far_first, 1):
        panels[mask] = swap(features, "loop", mask)

    mat_shape = (all_rows, row_count)
    mat_bytes = 2 * all_rows * row_count
    small = loop_count * mat_bytes <= 8 << 20
    late = [m ^ 1 for m in far_first]
    stay = [*far_first, 0]
    far_count = 0 if small else len(stay)
    graph = (dst_block[0, 0], src_block[0, 0], live_count[0], tiles[0, 0])
    sides = (features, degree[None, :], cotangent)

    def place(masks, far, packs):
        near_count = 0 if far else len(masks)
        kind = pltpu.HBM if far else jax.ShapeDtypeStruct
        bundle = [bf16((row_count + 16, feat_width + hidden))] if packs else []
        operands = graph + sides if packs else graph
        placed = pl.pallas_call(
            functools.partial(place_kernel, near_count, masks, rep_count, sub_blocks, packs),
            out_shape=[kind(mat_shape, jnp.bfloat16)] * len(masks) + bundle,
            in_specs=[HBM] * len(operands),
            out_specs=[HBM if far else VMEM] * len(masks) + [VMEM] * len(bundle),
            scratch_shapes=[pltpu.SMEM(g.shape, jnp.int32) for g in graph[:3]]
            + [
                pltpu.VMEM((len(masks), *mat_shape) if far else (1, 16, 128), jnp.bfloat16),
                pltpu.VMEM((1, row_count), jnp.int32),
                pltpu.SemaphoreType.DMA((6,)),
                pltpu.SemaphoreType.DMA((len(masks),)),
                pltpu.SemaphoreType.DMA((len(masks),)),
            ],
            compiler_params=pltpu.CompilerParams(vmem_limit_bytes=grant(len(masks) * mat_bytes)),
            cost_estimate=pl.CostEstimate(
                flops=0, bytes_accessed=2 * len(masks) * mat_bytes, transcendentals=0
            ),
        )(*map(in_hbm, operands))
        mats = [in_hbm(mat) if far else mat for mat in placed[: len(masks)]]
        return dict(zip(masks, mats)), placed[len(masks) :]

    away_masks = [*late, 1]
    mats, (bundle,) = place(away_masks + stay if small else away_masks, False, True)
    if not small:
        mats |= place(stay, True, False)[0]
    bundles = [bundle] + [swap(bundle, "rep", mask) for mask in range(2, rep_count, 2)]
    arrivals = [*far_first[:0:-1], far_first[0], 1]
    mats[late[0]], *got = after(mats[late[0]], *[panels[m] for m in arrivals])
    panels.update(zip(arrivals, got))
    for mask in arrivals[:-1]:
        panels[mask ^ 1] = swap(panels[mask], "loop", 1)

    early = [1, *stay]
    (running,) = pl.pallas_call(
        functools.partial(gather_first_kernel, len(early) - far_count, len(early)),
        out_shape=[f32((all_rows, feat_width))],
        in_specs=[VMEM] * (len(early) - far_count)
        + [HBM] * far_count
        + [VMEM] * len(early),
        out_specs=[VMEM],
        scratch_shapes=[
            pltpu.VMEM((far_count, *mat_shape) if far_count else (1, 16, 128), jnp.bfloat16),
            pltpu.SemaphoreType.DMA((2 * max(1, far_count),)),
        ],
        compiler_params=pltpu.CompilerParams(vmem_limit_bytes=grant(2 * loop_count * mat_bytes)),
        cost_estimate=pl.CostEstimate(
            flops=2 * len(early) * all_rows * row_count * feat_width,
            bytes_accessed=far_count * mat_bytes,
            transcendentals=0,
        ),
    )(*[mats[m] for m in early], *[panels[m] for m in early])
    *sooner, latest = [m ^ 1 for m in arrivals[:-1]]
    for mask in sooner:
        (running,) = call(
            gather_more_kernel,
            [f32((all_rows, feat_width))],
            [VMEM] * 3,
            (mats[mask], panels[mask], running),
        )
    keep, send = call(
        functools.partial(gather_last_kernel, 1),
        [f32((half_rows, feat_width)), bf16((half_rows, feat_width))],
        [VMEM] * 3,
        (mats[latest], panels[latest], running),
    )
    total = added(keep, swap(send, "rep", 1))
    total, *bundles = after(total, *bundles)
    mask = 2
    while True:
        term = swap(total, "rep", mask)
        if 2 * mask >= rep_count:
            break
        blocks = term.reshape(-1, 2, mask // 2 * row_count, feat_width)[:, ::-1]
        total = (
            total.astype(jnp.float32) + blocks.reshape(half_rows, feat_width).astype(jnp.float32)
        ).astype(jnp.bfloat16)
        mask *= 2

    scale = 1.0 / math.sqrt(row_count * loop_count * rep_count)
    weight_shape = (feat_width + 16, hidden)
    output_shape = (row_count, hidden)
    output, grad_pre, aggregate, grad_agg = call(
        functools.partial(middle_kernel, mask // 2),
        [
            bf16(output_shape),
            bf16((half_rows, hidden)),
            bf16((half_rows, feat_width)),
            bf16((half_rows, feat_width)),
        ],
        [VMEM] * (5 + len(bundles)),
        (total, term, w_self, w_neigh, bias[None, :], *bundles),
        flops=4 * half_rows * feat_width * hidden,
    )
    grad_far = swap(grad_agg, "rep", 1)
    keep_w, send_w = call(
        functools.partial(weight_kernel, scale),
        [f32(weight_shape)] * 2,
        [VMEM] * (2 + len(bundles)),
        (aggregate, grad_pre, *bundles),
        flops=4 * half_rows * feat_width * hidden,
    )
    sent_w = added(keep_w, swap(send_w, "rep", 1))

    away_groups = [1] * (len(far_first) - 1) + [2]
    begun = call(
        functools.partial(spread_near_kernel, len(away_masks)),
        [f32((feat_width, row_count))] * len(away_masks),
        [VMEM] * (len(away_masks) + 1),
        (*[mats[m] for m in away_masks], grad_agg),
        flops=len(stay) * all_rows * row_count * feat_width,
    )
    away = call(
        functools.partial(spread_away_kernel, away_groups),
        [bf16((size * row_count, feat_width)) for size in away_groups],
        [VMEM] * (2 * len(away_masks) + 1),
        (*[mats[m] for m in away_masks], *begun, grad_far),
        flops=len(stay) * all_rows * row_count * feat_width,
    )
    arrived = [swap(message, "loop", 1) for message in away]
    grad_far, *away = after(grad_far, *away)
    kept = pl.pallas_call(
        functools.partial(spread_here_kernel, len(stay) - far_count, len(stay)),
        out_shape=[bf16((row_count, feat_width))] * len(far_first)
        + [f32((row_count, feat_width)), pltpu.HBM(output_shape, jnp.bfloat16)],
        in_specs=[VMEM] * (len(stay) - far_count) + [HBM] * far_count + [VMEM] * 5,
        out_specs=[VMEM] * len(stay) + [HBM],
        scratch_shapes=[
            pltpu.VMEM((far_count, *mat_shape) if far_count else (1, 16, 128), jnp.bfloat16),
            pltpu.SemaphoreType.DMA((2 * max(1, far_count),)),
            pltpu.SemaphoreType.DMA,
        ],
        compiler_params=pltpu.CompilerParams(vmem_limit_bytes=grant(2 * loop_count * mat_bytes)),
        cost_estimate=pl.CostEstimate(
            flops=2 * len(stay) * all_rows * row_count * feat_width,
            bytes_accessed=far_count * mat_bytes,
            transcendentals=0,
        ),
    )(*[mats[m] for m in stay], grad_agg, grad_far, grad_pre, w_self, output)
    *kept, output = kept
    arrived_w = swap(sent_w, "loop", loop_count // 2)
    pieces = [(message, k) for message, size in zip(arrived, away_groups) for k in range(size)]
    pairs = []
    for term, (message, part) in zip(kept[:-1], pieces):
        pairs += call(
            functools.partial(pair_kernel, part),
            [bf16((row_count, feat_width))],
            [VMEM] * 2 + [pl.BlockSpec(memory_space=pl.ANY)] * len(pairs[-1:]),
            (term, message, *pairs[-1:]),
        )
    back = [swap(pair, "loop", m) for m, pair in zip(far_first, pairs)]
    mask = loop_count // 4
    while mask:
        sent_w = added(sent_w, arrived_w, *(pairs[2:3] if mask == 1 else kept[:1]))
        arrived_w = swap(sent_w, "loop", mask)
        mask //= 2
    sent_w = added(sent_w, arrived_w, token(back, 12_000_000_000), dtype=jnp.float32)
    message, part = pieces[-1]
    (grad_input,) = call(
        functools.partial(sum_kernel, part),
        [bf16((row_count, feat_width))],
        [VMEM] * (2 + len(back)),
        (kept[-1], message, *back),
    )
    other = swap(sent_w[:feat_width], "rep", 1)
    grad_self, grad_neigh, grad_bias = call(
        finish_kernel,
        [f32((feat_width, hidden)), f32((feat_width, hidden)), f32((1, hidden))],
        [VMEM] * 2,
        (sent_w, other),
    )
    return (output, grad_input, grad_self, grad_neigh, grad_bias[0])


def solution(mesh):
    in_specs = (
        P(("loop", "rep"), None),
        P(),
        P(),
        P(),
        P(("loop", "rep")),
        P("loop", "rep", None, None, None, None),
        P("loop", "rep", None, None),
        P("loop", "rep", None, None),
        P("loop", "rep", None),
        P(("loop", "rep"), None),
    )
    out_specs = (P(("loop", "rep"), None), P(("loop", "rep"), None), P(), P(), P())
    return jax.shard_map(
        per_device, mesh=mesh, in_specs=in_specs, out_specs=out_specs, check_vma=False
    )
```
